256 devices in a mesh: dom: 64 (over z_hi, x, y), band: 4 (over z_lo, core).
Axes of the slice: x: 4, y: 4, z: 8 (z_hi: 4, z_lo: 2; z = z_hi * 2 + z_lo), core: 2. Of those that a mesh axis runs over, the one named last changes fastest.
Arguments:
- wavefunctions: float32 [16384, 512], P('dom', 'band'), may hold values from -6 to 6
- node_mass: float32 [16384], P('dom'), may hold values from 1 to 2
- cell_potential: float32 [16384], P('dom'), may hold values from 0 to 2
- cell_nodes: int32 [8, 16384], P(None, 'dom'), may hold values from 0 to 319, as said below
- plane_nodes: int32 [4096], P('dom'), may hold values from 0 to 255, as said below
- state_order: int32 [512], replicated, may hold values from 0 to 511, each once
Outputs:
- filtered: float32 [16384, 512], P('dom', 'band')
- margin: float32 [512, 512], P('dom', 'band')
The draws below stay inside these ranges and needn't reach their ends.
Inputs may be any that keep to these rules, and one draw needn't show every extreme that they name: `cell_nodes`: in each partition, cell c has its corners in node layers c // 64 and c // 64 + 1. An entry below 256 is a row of the partition's own block; an entry 256 + q is the q-th node named by the next partition's plane_nodes. Only cells c >= 192 of a partition have such entries. Every own row is a corner of some cell. `plane_nodes`: each partition's 64 entries are distinct rows of its own block, all in its first node layer.
All inputs are finite; a program needn't handle non-finite values.
Results may differ from the reference program's by a relative error of at most 0.0001.
Values sent between devices are 32-bit elements; how exact they have to be, the bound alone decides.
No kernel may reach another device: no remote copies, remote signals or barrier semaphores. Data moves between devices by JAX's collectives and lax.ppermute only.
A program may use at most 64 MiB of HBM per device.

```python
import jax
import jax.numpy as jnp
import numpy as np
from jax import lax

LX = 4
PY = 8
PZ = 8
DEGREE = 8
PLANE = 64
NODE_DEV = 256
DOMS = 64
NODES = 16384
STATES = 512


def layout_slots(key):
    part_keys = jax.random.split(key, DOMS)
    orders = jax.vmap(lambda part_key: jax.random.permutation(part_key, NODE_DEV))(part_keys)
    return jnp.argsort(orders, axis=1).astype(jnp.int32)


def draw_cell_nodes(key, part):
    node_slots = layout_slots(key)
    canonical = jnp.arange(NODE_DEV, dtype=jnp.int32)
    layer_index = canonical // PLANE
    across_index = canonical // PZ % PY
    depth_index = canonical % PZ
    corner_list = []
    for corner in range(8):
        shift_x = corner // 4
        shift_y = corner // 2 % 2
        shift_z = corner % 2
        next_layer = layer_index + shift_x
        plane_slot = (across_index + shift_y) % PY * PZ + (depth_index + shift_z) % PZ
        inside_node = jnp.minimum(next_layer, LX - 1) * PLANE + plane_slot
        owned_slot = jnp.take(node_slots, inside_node, axis=1)
        ghost_slot = jnp.broadcast_to(NODE_DEV + plane_slot, owned_slot.shape)
        corner_list.append(jnp.where(next_layer < LX, owned_slot, ghost_slot))
    return jnp.stack(corner_list, 0).reshape(8, DOMS * NODE_DEV).astype(jnp.int32)


def draw_plane_nodes(key, part):
    node_slots = layout_slots(key)
    return node_slots[:, :PLANE].reshape(DOMS * PLANE).astype(jnp.int32)


def steps_of(stream_key, shape, cuts, least, largest):
    gain, own = 1.0, jax.random.fold_in(stream_key, 6)
    for dim, blocks in cuts:
        steps = jnp.exp(jax.random.uniform(jax.random.fold_in(own, dim), (blocks,), jnp.float32, least / len(cuts), largest / len(cuts)))
        gain = gain * jnp.repeat(steps, shape[dim] // blocks).reshape([-1 if axis == dim else 1 for axis in range(len(shape))])
    return gain


def centred(rng, shape, scale, most, shards=(), kind=jnp.bfloat16):
    factor_of = steps_of(rng, shape, shards, -0.22, 0.18) if shards else 1.0
    values = jax.random.normal(rng, shape, jnp.float32) * scale * factor_of
    return jnp.minimum(jnp.maximum(values, -most), most).astype(kind)


def setup_inputs(seed: int = 0) -> dict:
    keys = jax.random.split(jax.random.key(seed), 7)
    wavefunctions = centred(keys[0], (NODES, STATES), 1.0, 6.0, ((0, 64), (1, 4)), jnp.float32)
    node_mass = jnp.clip(1.0 + 1.0 * jax.random.uniform(keys[1], (NODES,), jnp.float32) ** steps_of(keys[1], (NODES,), ((0, 64),), -0.2, 0.2), 1.0, 2.0)
    cell_potential = jnp.clip(2.0 * jax.random.uniform(keys[2], (NODES,), jnp.float32) ** steps_of(keys[2], (NODES,), ((0, 64),), -0.2, 0.2), 0.0, 2.0)
    cell_nodes = draw_cell_nodes(jax.random.fold_in(keys[6], 71), 0)
    plane_nodes = draw_plane_nodes(jax.random.fold_in(keys[6], 71), 0)
    state_order = jax.random.permutation(keys[5], STATES).astype(jnp.int32)
    return dict(wavefunctions=wavefunctions, node_mass=node_mass, cell_potential=cell_potential, cell_nodes=cell_nodes, plane_nodes=plane_nodes, state_order=state_order)


lower_cut = 1.5
upper_edge = 5.0
anchor_value = 0.4

def cell_tables():
    stiff_line = np.array([[1.0, -1.0], [-1.0, 1.0]])
    mass_line = np.array([[1.0 / 3.0, 1.0 / 6.0], [1.0 / 6.0, 1.0 / 3.0]])
    stiffness = np.kron(np.kron(stiff_line, mass_line), mass_line)
    stiffness = stiffness + np.kron(np.kron(mass_line, stiff_line), mass_line)
    stiffness = stiffness + np.kron(np.kron(mass_line, mass_line), stiff_line)
    cell_mass = np.kron(np.kron(mass_line, mass_line), mass_line)
    return np.concatenate([0.5 * stiffness, cell_mass], 0).astype(np.float32)

def local_apply(owned, ghost_plane, links, potential, cell_table):
    extended = jnp.concatenate([owned, ghost_plane], 0)
    state_width = owned.shape[1]
    cell_count = links.shape[1]
    gathered = extended[links.reshape(-1)].reshape(8, cell_count * state_width)
    mixed = jnp.dot(cell_table, gathered, precision=lax.Precision.HIGHEST, preferred_element_type=jnp.float32).reshape(16, cell_count, state_width)
    contrib = mixed[:8] + potential[None, :, None] * mixed[8:]
    result = jnp.zeros((owned.shape[0] + ghost_plane.shape[0], state_width), jnp.float32)
    return result.at[links.reshape(-1)].add(contrib.reshape(-1, state_width))

def assembled(field_values, cell_nodes, cell_potential, plane_nodes, cell_table):
    parts = field_values.reshape(DOMS, NODE_DEV, -1)
    bounds = plane_nodes.reshape(DOMS, PLANE).astype(jnp.int32)
    planes = jax.vmap(lambda owned, picks: owned[picks])(parts, bounds)
    ghosts = jnp.concatenate([planes[1:], jnp.zeros_like(planes[:1])], 0)
    linkage = cell_nodes.reshape(8, DOMS, NODE_DEV).transpose(1, 0, 2)
    potentials = cell_potential.reshape(DOMS, NODE_DEV)

    def one_part(items):
        return local_apply(items[0], items[1], items[2], items[3], cell_table)
    outputs = lax.map(one_part, (parts, ghosts, linkage, potentials))
    carried = jnp.concatenate([jnp.zeros_like(outputs[:1, NODE_DEV:]), outputs[:-1, NODE_DEV:]], 0)
    result = jax.vmap(lambda owned, picks, extra: owned.at[picks].add(extra))(outputs[:, :NODE_DEV], bounds, carried)
    return result.reshape(NODES, -1)

def reference(wavefunctions, node_mass, cell_potential, cell_nodes, plane_nodes, state_order):
    cell_table = jnp.asarray(cell_tables(), jnp.float32)
    node_scale = lax.rsqrt(node_mass)[:, None]

    def hamiltonian(field_values):
        return node_scale * assembled(node_scale * field_values, cell_nodes, cell_potential, plane_nodes, cell_table)
    half_span = (upper_edge - lower_cut) / 2.0
    center = (upper_edge + lower_cut) / 2.0
    sigma_first = half_span / (anchor_value - center)
    gamma_value = 2.0 / sigma_first
    previous = wavefunctions
    current = sigma_first / half_span * (hamiltonian(previous) - center * previous)
    sigma_last = sigma_first
    for degree_index in range(2, DEGREE + 1):
        sigma_next = 1.0 / (gamma_value - sigma_last)
        following = 2.0 * sigma_next / half_span * (hamiltonian(current) - center * current)
        following = following - sigma_last * sigma_next * previous
        previous = current
        current = following
        sigma_last = sigma_next
    filtered = current
    permuted = filtered[:, state_order]
    margin = jnp.dot(permuted.T, permuted, precision=lax.Precision.HIGHEST, preferred_element_type=jnp.float32) / NODES
    return (filtered, margin)
```

```python
import jax
import jax.numpy as jnp
import numpy as np
from jax import lax
from jax.experimental import pallas as pl
from jax.experimental.pallas import tpu as pltpu
from jax.sharding import PartitionSpec as P

DEGREE = 8
REACH = 2
WINDOW = 2 * REACH + 1

lower_cut = 1.5
upper_edge = 5.0
anchor_value = 0.4

half_span = (upper_edge - lower_cut) / 2.0
center = (upper_edge + lower_cut) / 2.0

VMEM = pl.BlockSpec(memory_space=pltpu.VMEM)
SMEM = pl.BlockSpec(memory_space=pltpu.SMEM)
f32 = jnp.float32
bf16 = jnp.bfloat16


def dot(a, b):
    return lax.dot_general(a, b, (((1,), (0,)), ((), ())), preferred_element_type=f32)


def dot_t(a, b):
    return lax.dot_general(a, b, (((1,), (1,)), ((), ())), preferred_element_type=f32)


def split(x):
    high = x.astype(bf16)
    return high, (x - high.astype(f32)).astype(bf16)


def corner_mix(corners, potential):
    total = corners[0]
    for item in corners[1:]:
        total = total + item
    mass = list(corners)
    for bit in (1, 2, 4):
        mixed = [None] * 8
        for a in range(8):
            if not a & bit:
                pair = mass[a] + mass[a | bit]
                mixed[a] = mass[a] + pair
                mixed[a | bit] = mass[a | bit] + pair
        mass = mixed
    result = []
    for a in range(8):
        near = corners[a ^ 1] + corners[a ^ 2] + corners[a ^ 4]
        stiff = 5 * corners[a] + near - total
        result.append(stiff.astype(f32) * (1.0 / 24.0) + mass[a].astype(f32) * (potential * (1.0 / 216.0)))
    return result


def build_kernel(place, own, r1, l1, r2, l2, high_ref, low_ref, nn_ref):
    position, last = place[0], place[2]
    blocks = {REACH - 2: l2, REACH - 1: l1, REACH: own, REACH + 1: r1, REACH + 2: r2}
    nodes = own.shape[1]
    row_id = lax.broadcasted_iota(jnp.int32, (nodes, nodes), 0).astype(f32)
    col_id = lax.broadcasted_iota(jnp.int32, (nodes, nodes), 1).astype(f32)
    diagonal = row_id == col_id
    ghost_id = row_id[:128, :128] + float(nodes)

    def exists(q):
        where = position + (q - REACH)
        return jnp.logical_and(where >= 0, where <= last)

    scale_row, scale_col = [], []
    for q in range(WINDOW):
        mass = jnp.where(exists(q), blocks[q][9:10, :], 1.0)
        row = lax.rsqrt(mass)
        scale_row.append(row)
        scale_col.append(jnp.sum(jnp.where(diagonal, row, 0.0), axis=1, keepdims=True))
    for q in range(WINDOW):
        block = blocks[q]
        potential = block[8:9, :]
        corners = [jnp.where(row_id == block[a : a + 1, :], 1.0, 0.0).astype(bf16) for a in range(8)]
        mixed = corner_mix(corners, potential)
        own_own = jnp.zeros((nodes, nodes), f32)
        for a in range(8):
            high, low = split(mixed[a])
            own_own = own_own + dot_t(corners[a], high) + dot_t(corners[a], low)
        if q > 0:
            own_own = own_own + nn_ref[...]
        mid = own_own * (scale_col[q] * (1.0 / half_span)) * scale_row[q]
        mid = mid - jnp.where(diagonal, center / half_span, 0.0)
        high, low = split(mid)
        high_ref[q, :, nodes : 2 * nodes] = high
        low_ref[q, :, nodes : 2 * nodes] = low
        if q + 1 < WINDOW:
            joined = jnp.where(jnp.logical_and(exists(q), exists(q + 1)), 1.0, 0.0)
            tail = nodes - 128
            ghosts = [
                jnp.where(ghost_id == block[a : a + 1, tail:], 1.0, 0.0).astype(bf16) for a in range(8)
            ]
            ghost_mixed = corner_mix(ghosts, potential[:, tail:])
            og = jnp.zeros((nodes, 128), f32)
            gg = jnp.zeros((128, 128), f32)
            for a in range(8):
                high, low = split(ghost_mixed[a])
                tail_corner = corners[a][:, tail:]
                og = og + dot_t(tail_corner, high) + dot_t(tail_corner, low)
                gg = gg + dot_t(ghosts[a], high) + dot_t(ghosts[a], low)
            og = og * joined
            gg = gg * joined
            place_next = jnp.where(row_id[:, :128] == blocks[q + 1][10:11, :128], 1.0, 0.0).astype(bf16)
            og_high, og_low = split(og)
            up = dot_t(og_high, place_next) + dot_t(og_low, place_next)
            down = dot_t(place_next, og_high) + dot_t(place_next, og_low)
            gg_high, gg_low = split(gg)
            half_high = dot(place_next, gg_high).astype(bf16)
            half_low = dot(place_next, gg_low).astype(bf16)
            nn_ref[...] = dot_t(half_high, place_next) + dot_t(half_low, place_next)
            up = up * (scale_col[q] * (1.0 / half_span)) * scale_row[q + 1]
            down = down * (scale_col[q + 1] * (1.0 / half_span)) * scale_row[q]
            high, low = split(up)
            high_ref[q, :, 2 * nodes :] = high
            low_ref[q, :, 2 * nodes :] = low
            high, low = split(down)
            high_ref[q + 1, :, :nodes] = high
            low_ref[q + 1, :, :nodes] = low


def filter_kernel(place, own, near_a, near_b, far_a, far_b, high_ref, low_ref, out, even, odd, field_a, field_b):
    position = place[0]
    nodes, width = own.shape
    is_even = lax.rem(position, 2) == 0
    is_low = lax.rem(position, 4) < 2
    first = [
        jnp.where(is_low, far_b[...], far_a[...]),
        jnp.where(is_even, near_b[...], near_a[...]),
        own[...],
        jnp.where(is_even, near_a[...], near_b[...]),
        jnp.where(is_low, far_a[...], far_b[...]),
    ]

    def put(target, q, value):
        high, low = split(value)
        target[nodes * q : nodes * (q + 1), :width] = high
        target[nodes * q : nodes * (q + 1), width:] = low

    for q in range(WINDOW):
        field_a[q] = first[q]
        put(even, q, first[q])
    sigma_first = half_span / (anchor_value - center)
    gamma_value = 2.0 / sigma_first
    sigma_last = sigma_first
    layers = 4
    for k in range(1, DEGREE + 1):
        source, target = (even, odd) if k % 2 else (odd, even)
        older, newer = (field_a, field_b) if k % 2 else (field_b, field_a)
        if k == 1:
            gain, keep = sigma_first, None
        else:
            sigma_next = 1.0 / (gamma_value - sigma_last)
            gain, keep = 2.0 * sigma_next, sigma_last * sigma_next
            sigma_last = sigma_next
        reach = -(-(DEGREE - k) // layers)
        for q in range(REACH - reach, REACH + reach + 1):
            start, stop = max(q - 1, 0), min(q + 2, WINDOW)
            left, right = nodes * (start - q + 1), nodes * (stop - q + 1)
            rows = slice(nodes * start, nodes * stop)
            main = dot(high_ref[q, :, left:right], source[rows, :])
            rest = dot(low_ref[q, :, left:right], source[rows, :width])
            value = gain * (main[:, :width] + main[:, width:] + rest)
            if keep is not None:
                value = value - keep * newer[q]
            if k == DEGREE:
                out[...] = value
            else:
                newer[q] = value
                put(target, q, value)


def margin_kernel(place, states, order, out):
    band = place[1]
    count = order.shape[1]
    width = out.shape[1]
    state_id = lax.broadcasted_iota(jnp.int32, (count, count), 0)
    pick = jnp.where(state_id == order[...], 1.0, 0.0).astype(bf16)
    high, low = split(states[...])
    high = dot(high, pick)
    low = dot(low, pick).astype(bf16)
    high = high.astype(bf16)
    own_order = order[:, pl.ds(pl.multiple_of(band * width, width), width)]
    own_pick = jnp.where(state_id[:, :width] == own_order, 1.0, 0.0).astype(bf16)
    own_high, own_low = split(states[...])
    own_high = dot(own_high, own_pick).astype(bf16)
    own_low = dot(own_low, own_pick).astype(bf16)

    def cross(a, b):
        return lax.dot_general(a, b, (((0,), (0,)), ((), ())), preferred_element_type=f32)

    out[...] = cross(high, own_high) + cross(high, own_low) + cross(low, own_high)


def swapped(block, axis, pairs):
    count = lax.axis_size(axis)
    route = [
        step for a, b in pairs if a < count and b < count for step in ((a, b), (b, a))
    ]
    return lax.ppermute(block, axis, route)


def shards(wavefunctions, node_mass, cell_potential, cell_nodes, plane_nodes, state_order):
    nodes, width = wavefunctions.shape
    doms = lax.axis_size("dom")
    place = jnp.stack([lax.axis_index("dom"), lax.axis_index("band"), doms - 1]).astype(jnp.int32)
    position = lax.axis_index("dom")
    plane_row = jnp.pad(plane_nodes.astype(f32), (0, nodes - plane_nodes.shape[0]), constant_values=-1.0)
    small = jnp.concatenate(
        [
            cell_nodes.astype(f32),
            cell_potential[None, :],
            node_mass[None, :],
            plane_row[None, :],
            jnp.zeros((5, nodes), f32),
        ],
        0,
    )
    near_pairs = [
        [(2 * i, 2 * i + 1) for i in range(doms)],
        [(2 * i + 1, 2 * i + 2) for i in range(doms)],
    ]
    far_pairs = [
        [(4 * i + j, 4 * i + j + 2) for i in range(doms) for j in range(2)],
        [(4 * i + j + 2, 4 * i + j + 4) for i in range(doms) for j in range(2)],
    ]
    routes = near_pairs + far_pairs
    small_got = [swapped(small, "dom", route) for route in routes]
    field_got = [swapped(wavefunctions, "dom", route) for route in routes]
    is_even = position % 2 == 0
    is_low = position % 4 < 2
    small_r1 = jnp.where(is_even, small_got[0], small_got[1])
    small_l1 = jnp.where(is_even, small_got[1], small_got[0])
    small_r2 = jnp.where(is_low, small_got[2], small_got[3])
    small_l2 = jnp.where(is_low, small_got[3], small_got[2])

    high, low = pl.pallas_call(
        build_kernel,
        out_shape=[jax.ShapeDtypeStruct((WINDOW, nodes, 3 * nodes), bf16)] * 2,
        in_specs=[SMEM] + [VMEM] * 5,
        out_specs=[VMEM] * 2,
        scratch_shapes=[pltpu.VMEM((nodes, nodes), f32)],
        compiler_params=pltpu.CompilerParams(vmem_limit_bytes=40 * 2**20),
        cost_estimate=pl.CostEstimate(flops=8_000_000_000, bytes_accessed=4_000_000, transcendentals=0),
        name="build",
    )(place, small, small_r1, small_l1, small_r2, small_l2)

    filtered = pl.pallas_call(
        filter_kernel,
        out_shape=jax.ShapeDtypeStruct((nodes, width), f32),
        in_specs=[SMEM] + [VMEM] * 7,
        out_specs=VMEM,
        scratch_shapes=[
            pltpu.VMEM((WINDOW * nodes, 2 * width), bf16),
            pltpu.VMEM((WINDOW * nodes, 2 * width), bf16),
            pltpu.VMEM((WINDOW, nodes, width), f32),
            pltpu.VMEM((WINDOW, nodes, width), f32),
        ],
        compiler_params=pltpu.CompilerParams(vmem_limit_bytes=40 * 2**20),
        cost_estimate=pl.CostEstimate(flops=6_000_000_000, bytes_accessed=5_000_000, transcendentals=0),
        name="filter",
    )(place, wavefunctions, *field_got, high, low)

    all_states = lax.all_gather(filtered, "band", axis=1, tiled=True)
    term = pl.pallas_call(
        margin_kernel,
        out_shape=jax.ShapeDtypeStruct((state_order.shape[0], width), f32),
        in_specs=[SMEM, VMEM, VMEM],
        out_specs=VMEM,
        compiler_params=pltpu.CompilerParams(vmem_limit_bytes=40 * 2**20),
        name="margin",
    )(place, all_states, state_order[None, :])
    rows = state_order.shape[0] // doms
    parts = lax.all_to_all(term.reshape(doms, rows, width), "dom", 0, 0, tiled=True)
    return (filtered, parts.sum(0) * (1.0 / (nodes * doms)))


def solution(mesh):
    in_specs = (P("dom", "band"), P("dom"), P("dom"), P(None, "dom"), P("dom"), P())
    out_specs = (P("dom", "band"), P("dom", "band"))
    return jax.shard_map(shards, mesh=mesh, in_specs=in_specs, out_specs=out_specs, check_vma=False)
```

```python
import jax
import jax.numpy as jnp
import numpy as np
from jax import lax
from jax.experimental import pallas as pl
from jax.experimental.pallas import tpu as pltpu
from jax.sharding import PartitionSpec as P

DEGREE = 8
REACH = 2
WINDOW = 2 * REACH + 1
LAYERS = 4
EXTRA = 24

lower_cut = 1.5
upper_edge = 5.0
anchor_value = 0.4

half_span = (upper_edge - lower_cut) / 2.0
center = (upper_edge + lower_cut) / 2.0
sigma_first = half_span / (anchor_value - center)
gamma_value = 2.0 / sigma_first


VMEM = pl.BlockSpec(memory_space=pltpu.VMEM)
SMEM = pl.BlockSpec(memory_space=pltpu.SMEM)
ANY = pl.BlockSpec(memory_space=pl.ANY)
f32 = jnp.float32
bf16 = jnp.bfloat16


def dot(a, b):
    return lax.dot_general(a, b, (((1,), (0,)), ((), ())), preferred_element_type=f32)


def dot_t(a, b):
    return lax.dot_general(a, b, (((1,), (1,)), ((), ())), preferred_element_type=f32)


def split(x):
    high = x.astype(bf16)
    return high, (x - high.astype(f32)).astype(bf16)


def coarse_parts(x):
    parts = []
    for _ in range(3):
        scaled = x * float(2**19 + 1)
        part = scaled - (scaled - x)
        parts.append(part)
        x = x - part
    return parts


def exact(x):
    high, rest = x.astype(bf16), x
    terms = [high]
    for _ in range(2):
        rest = rest - terms[-1].astype(f32)
        terms.append(rest.astype(bf16))
    return terms


def cross(a, b):
    return lax.dot_general(a, b, (((0,), (0,)), ((), ())), preferred_element_type=f32)


def iota(shape, dim):
    return lax.broadcasted_iota(jnp.int32, shape, dim)


def flag(mask):
    return jnp.where(mask, 1.0, 0.0).astype(bf16)


def column_of(row):
    count = row.shape[1]
    terms = jnp.concatenate([t.astype(f32) for t in exact(row)] + [jnp.zeros((13, count), f32)], 0)
    return cross(terms.astype(bf16), jnp.ones((16, 128), bf16))


def sort_kernel(field, links, potential, mass, plane, out, rank_out, field_in, links_in, rows_in, plane_in, sems):
    nodes, width = field.shape
    copies = [
        pltpu.make_async_copy(field, field_in, sems.at[0]),
        pltpu.make_async_copy(links, links_in, sems.at[1]),
        pltpu.make_async_copy(potential, rows_in.at[pl.ds(0, 1)], sems.at[2]),
        pltpu.make_async_copy(mass, rows_in.at[pl.ds(1, 1)], sems.at[3]),
        pltpu.make_async_copy(plane, plane_in, sems.at[4]),
    ]
    for copy in copies:
        copy.start()
    for copy in copies[1:]:
        copy.wait()
    corners = links_in[...]
    corner_id = corners.astype(f32)
    plane_count = plane.shape[1]
    plane_row = jnp.concatenate([plane_in[...].astype(f32), jnp.full((1, 128 - plane_count), -1.0, f32)], 1)

    row_id = iota((nodes, nodes), 0).astype(f32)
    lane_id = iota((nodes, nodes), 1).astype(f32)
    row_small = row_id.astype(bf16)
    touched = None
    for a in range(8):
        hits = jnp.where(row_small == corner_id[a : a + 1, :].astype(bf16), jnp.ones_like(row_small), jnp.zeros_like(row_small))
        touched = hits if touched is None else touched + hits
    span = nodes // LAYERS
    by_layer = flag(iota((nodes, 128 * LAYERS), 0) // span == iota((nodes, 128 * LAYERS), 1) // 128)
    counts = dot(touched, by_layer)
    layer = [counts[:, 128 * i : 128 * (i + 1)] > 0.5 for i in range(LAYERS)]
    in_plane = flag(row_id[:, :128] == plane_row)
    is_plane = dot(in_plane, jnp.ones((128, 128), bf16)) > 0.5
    least = jnp.where(layer[0], 0.0, jnp.where(layer[1], 1.0, jnp.where(layer[2], 2.0, 3.0)))
    most = jnp.where(layer[3], 3.0, jnp.where(layer[2], 2.0, jnp.where(layer[1], 1.0, 0.0)))
    key = jnp.where(is_plane, -1.0, least + most)
    key_row = cross(key.astype(bf16), flag(row_id == lane_id))[0:1, :]
    order_col = key * float(nodes) + row_id[:, :128]
    order_row = key_row * float(nodes) + lane_id[0:1, :]
    before = flag(jnp.concatenate([order_col] * (nodes // 128), 1) < order_row)
    counted = dot(jnp.ones((16, nodes), bf16), before)[0:1, :]
    sub = iota((16, 128), 0)
    plane_facts = dot_t(
        jnp.where(sub == 0, 1.0, jnp.where(sub == 1, iota((16, 128), 1).astype(f32), 0.0)).astype(bf16), in_plane
    )
    rank = jnp.where(plane_facts[0:1, :] > 0.5, plane_facts[1:2, :], counted)
    rank_out[...] = jnp.broadcast_to(rank, rank_out.shape)

    low_lane = iota((8, 128), 1) < 64
    ranks = [jnp.broadcast_to(rank[:, 128 * h : 128 * (h + 1)], (8, 128)) for h in range(2)]
    for m in range(2):
        part = corners[:, 128 * m : 128 * (m + 1)]
        local = lax.bitwise_and(part, 127)
        found = [jnp.take_along_axis(r, local, axis=1) for r in ranks]
        place = jnp.where(part < 128, found[0], jnp.where(part < nodes, found[1], part.astype(f32)))
        place = place - jnp.where(low_lane, 128.0 * m, 128.0 * m + 64.0)
        turned = pltpu.roll(place, 64, 1)
        chance = rows_in[0:1, 128 * m : 128 * (m + 1)]
        chance = jnp.broadcast_to(chance, (8, 128))
        chance_turned = pltpu.roll(chance, 64, 1)
        for i in range(4):
            even, odd = slice(2 * i, 2 * i + 1), slice(2 * i + 1, 2 * i + 2)
            at = nodes + 8 * m + i
            out[at : at + 1, :] = jnp.where(low_lane[0:1], place[even], turned[odd])
            out[at + 4 : at + 5, :] = jnp.where(low_lane[0:1], turned[even], place[odd])
        at = nodes + 16 + 2 * m
        out[at : at + 1, :] = jnp.where(low_lane, chance, chance_turned)[0:1]
        out[at + 1 : at + 2, :] = jnp.where(low_lane, chance_turned, chance)[0:1]

    move = flag(row_id == rank)
    scale = lax.rsqrt(rows_in[1:2, :])
    terms = jnp.concatenate([t.astype(f32) for t in exact(scale)] + [jnp.zeros((13, nodes), f32)], 0)
    moved = dot_t(terms.astype(bf16), move)
    scale = moved[0:1] + moved[1:2] + moved[2:3]
    out[nodes + 20 : nodes + 21, :] = scale[:, :128]
    out[nodes + 21 : nodes + 22, :] = scale[:, 128:]
    out[nodes + 22 : nodes + 24, :] = jnp.zeros((2, 128), f32)
    copies[0].wait()
    sorted_field = dot(move, jnp.concatenate(exact(field_in[...]), 1))
    sorted_field = sorted_field[:, :width] + sorted_field[:, width : 2 * width] + sorted_field[:, 2 * width :]
    out[:nodes, :] = sorted_field * column_of(scale)


def layer_matrix(table, layer, scratch):
    plain, pair, third = scratch
    low_lane = iota((1, 128), 1) < 64
    chance = table[16 + layer : 17 + layer, :]
    stiff = (0.0, 1.0 / 2.0, 1.0 / 3.0, 1.0 / 6.0)
    mass = (1.0 / 8.0, 1.0 / 24.0, 1.0 / 72.0, 1.0 / 216.0)
    whole = [(0.5 * k + chance * m) * 0.125 for k, m in zip(stiff, mass)]

    def spread(row):
        return jnp.broadcast_to(row, (16, 128)).astype(bf16)

    weights = [
        [spread(part) for part in coarse_parts(jnp.where(low_lane, whole[j], whole[j + 1]))] for j in range(3)
    ]
    rows = table[4 * layer : 4 * layer + 4, :]
    turned = pltpu.roll(table[8 * (layer // 2) : 8 * (layer // 2) + 8, :], 64, 1)
    turned = turned[4 * (layer % 2) : 4 * (layer % 2) + 4, :]
    straight = [spread(rows[i : i + 1, :]) for i in range(4)]
    opposite = [spread(turned[i : i + 1, :]) for i in range(4)]
    sign = spread(jnp.where(low_lane, 1.0, -1.0))
    one, zero = jnp.ones((16, 128), bf16), jnp.zeros((16, 128), bf16)
    for r in range(8):
        local = (iota((16, 128), 0) + 16 * r).astype(f32).astype(bf16)
        items = [
            jnp.where(local == s, sign, zero) + jnp.where(local == o, one, zero) for s, o in zip(straight, opposite)
        ]
        for bit in (1, 2):
            mixed = [None] * 4
            for i in range(4):
                if not i & bit:
                    mixed[i] = items[i] + items[i | bit]
                    mixed[i | bit] = items[i] - items[i | bit]
            items = mixed
        for i in range(4):
            part = weights[bin(i).count("1")]
            lanes = slice(128 * i, 128 * (i + 1))
            plain[16 * r : 16 * r + 16, lanes] = items[i]
            pair[16 * r : 16 * r + 16, lanes] = items[i] * part[0]
            pair[128 + 16 * r : 128 + 16 * r + 16, lanes] = items[i] * part[1]
            third[16 * r : 16 * r + 16, lanes] = items[i] * part[2]
    both = dot_t(plain[...], pair[...])
    return both[:, :128] + both[:, 128:] + dot_t(plain[...], third[...])


def partition_matrices(table, scratch, layers, out, first):
    for layer in layers:
        out[first + layer] = layer_matrix(table, layer, [ref.at[layer] for ref in scratch])


def own_kernel(packed, out, *scratch):
    partition_matrices(packed[packed.shape[0] - EXTRA :, :], scratch, range(LAYERS), out, 0)


def sides(choose, got_a, got_b, part):
    a, b = got_a[part, :], got_b[part, :]
    return jnp.where(choose, b, a), jnp.where(choose, a, b)


def near_kernel(place, got_a, got_b, out, *scratch):
    is_even = lax.rem(place[0], 2) == 0
    nodes = got_a.shape[0] - EXTRA
    for i, table in enumerate(sides(is_even, got_a, got_b, slice(nodes, nodes + EXTRA))):
        partition_matrices(table, scratch, range(LAYERS), out, LAYERS * i)


def filter_kernel(place, packed, near_a, near_b, far_a, far_b, rank_ref, own_cells, near_cells,
                  out, far_cells, bands, even, odd, field_a, field_b, *scratch):
    position = place[0]
    nodes, width = out.shape
    span = nodes // LAYERS
    table_part, field_part = slice(nodes, nodes + EXTRA), slice(0, nodes)
    is_even = lax.rem(position, 2) == 0
    is_low = lax.rem(position, 4) < 2
    left1, right1 = sides(is_even, near_a, near_b, table_part)
    left2, right2 = sides(is_low, far_a, far_b, table_part)
    tables = (left2, left1, packed[table_part, :], right1, right2)
    partition_matrices(left2, scratch, range(LAYERS), far_cells, 0)
    partition_matrices(right2, scratch, range(LAYERS - 1), far_cells, LAYERS)
    cells = [far_cells[i] for i in range(4)] + [near_cells[i] for i in range(4)] + [own_cells[i] for i in range(4)]
    cells += [near_cells[4 + i] for i in range(4)] + [far_cells[4 + i] for i in range(3)] + [None]

    low_lane = iota((128, 128), 1) < span
    on_first = iota((128, 128), 1) == iota((128, 128), 0) + span
    on_second = iota((128, 128), 1) == iota((128, 128), 0) - span
    blank = jnp.zeros((span, 128), f32)
    pairs = len(cells) // 2
    for q in range(WINDOW):
        scale = column_of(jnp.concatenate([tables[q][20:21], tables[q][21:22]], 1))
        weight = scale * scale * (1.0 / half_span)
        for j in (2 * q, 2 * q + 1):
            rows = slice(128 * (j - 2 * q), 128 * (j - 2 * q) + 128)
            turned = pltpu.roll(cells[2 * j], 64, 1)
            upper = blank if j == 0 else cells[2 * j - 1][span:, :]
            lower = blank if cells[2 * j + 1] is None else cells[2 * j + 1][:span, :]
            first = jnp.concatenate([upper, blank], 0) + jnp.where(low_lane, 0.0, turned)
            second = jnp.concatenate([blank, lower], 0) + jnp.where(low_lane, turned, 0.0)
            first = first * weight[rows, :] - jnp.where(on_first, center / half_span, 0.0)
            second = second * weight[rows, :] - jnp.where(on_second, center / half_span, 0.0)
            for lanes, value in ((slice(0, 128), first), (slice(128, 256), second)):
                high, low = split(value)
                bands[j, :128, lanes] = high
                bands[j, 128:, lanes] = low

    def put(target, at, value):
        count = value.shape[0]
        high, low = split(value)
        target[span + at : span + at + count, :width] = high
        target[span + at : span + at + count, width:] = low

    for target in (even, odd):
        target[:span, :] = jnp.zeros((span, 2 * width), bf16)
        target[span + WINDOW * nodes :, :] = jnp.zeros((span, 2 * width), bf16)
    field1 = sides(is_even, near_a, near_b, field_part)
    field2 = sides(is_low, far_a, far_b, field_part)
    for q, value in enumerate((field2[0], field1[0], packed[field_part, :], field1[1], field2[1])):
        field_a[nodes * q : nodes * (q + 1), :] = value
        put(even, nodes * q, value)
    sigma_last = sigma_first
    final = []
    for k in range(1, DEGREE + 1):
        source, target = (even, odd) if k % 2 else (odd, even)
        newer = field_b if k % 2 else field_a
        if k == 1:
            gain, keep = sigma_first, None
        else:
            sigma_next = 1.0 / (gamma_value - sigma_last)
            gain, keep = 2.0 * sigma_next, sigma_last * sigma_next
            sigma_last = sigma_next
        for j in range(k // 2, pairs - k // 2):
            product = dot(bands[j], source[128 * j : 128 * j + 256, :])
            value = gain * (product[:128, :width] + (product[:128, width:] + product[128:, :width]))
            if keep is not None:
                value = value - keep * newer[128 * j : 128 * (j + 1), :]
            if k == DEGREE:
                final.append(value)
            else:
                newer[128 * j : 128 * (j + 1), :] = value
                put(target, 128 * j, value)
    scale = column_of(jnp.concatenate([tables[REACH][20:21], tables[REACH][21:22]], 1))
    result = jnp.concatenate(final, 0) / scale
    move = flag(iota((nodes, nodes), 0).astype(f32) == rank_ref[0:1, :])
    back = cross(move, jnp.concatenate(exact(result), 1))
    out[...] = back[:, :width] + back[:, width : 2 * width] + back[:, 2 * width :]


def margin_kernel(place, states, order, out):
    band = place[1]
    count = order.shape[1]
    width = out.shape[1]
    state_id = lax.broadcasted_iota(jnp.int32, (count, count), 0)
    pick = jnp.where(state_id == order[...], 1.0, 0.0).astype(bf16)
    high, low = split(states[...])
    high = dot(high, pick)
    low = dot(low, pick).astype(bf16)
    high = high.astype(bf16)
    own_order = order[:, pl.ds(pl.multiple_of(band * width, width), width)]
    own_pick = jnp.where(state_id[:, :width] == own_order, 1.0, 0.0).astype(bf16)
    own_high, own_low = split(states[...])
    own_high = dot(own_high, own_pick).astype(bf16)
    own_low = dot(own_low, own_pick).astype(bf16)

    def cross(a, b):
        return lax.dot_general(a, b, (((0,), (0,)), ((), ())), preferred_element_type=f32)

    out[...] = cross(high, own_high) + cross(high, own_low) + cross(low, own_high)


def swapped(block, axis, pairs):
    count = lax.axis_size(axis)
    route = [
        step for a, b in pairs if a < count and b < count for step in ((a, b), (b, a))
    ]
    return lax.ppermute(block, axis, route)


def shards(wavefunctions, node_mass, cell_potential, cell_nodes, plane_nodes, state_order):
    nodes, width = wavefunctions.shape
    doms = lax.axis_size("dom")
    place = jnp.stack([lax.axis_index("dom"), lax.axis_index("band")]).astype(jnp.int32)
    near_pairs = [
        [(2 * i, 2 * i + 1) for i in range(doms)],
        [(2 * i + 1, 2 * i + 2) for i in range(doms)],
    ]
    far_pairs = [
        [(4 * i + j, 4 * i + j + 2) for i in range(doms) for j in range(2)],
        [(4 * i + j + 2, 4 * i + j + 4) for i in range(doms) for j in range(2)],
    ]
    params = pltpu.CompilerParams(vmem_limit_bytes=40 * 2**20)
    plane_count = plane_nodes.shape[0]

    packed, rank = pl.pallas_call(
        sort_kernel,
        out_shape=[jax.ShapeDtypeStruct((nodes + EXTRA, width), f32), jax.ShapeDtypeStruct((8, nodes), f32)],
        in_specs=[ANY] * 5,
        out_specs=[VMEM] * 2,
        scratch_shapes=[
            pltpu.VMEM((nodes, width), f32),
            pltpu.VMEM((8, nodes), jnp.int32),
            pltpu.VMEM((2, nodes), f32),
            pltpu.VMEM((1, plane_count), jnp.int32),
            pltpu.SemaphoreType.DMA((5,)),
        ],
        compiler_params=pltpu.CompilerParams(vmem_limit_bytes=60 * 2**20),
        name="sort",
    )(wavefunctions, cell_nodes, cell_potential[None, :], node_mass[None, :], plane_nodes[None, :])
    near_b, far_b, near_a, far_a = [
        swapped(packed, "dom", pairs)
        for pairs in (near_pairs[1], far_pairs[1], near_pairs[0], far_pairs[0])
    ]
    incidence = [
        pltpu.VMEM((LAYERS, 128, 512), bf16),
        pltpu.VMEM((LAYERS, 256, 512), bf16),
        pltpu.VMEM((LAYERS, 128, 512), bf16),
    ]
    own_cells = pl.pallas_call(
        own_kernel,
        out_shape=jax.ShapeDtypeStruct((LAYERS, 128, 128), f32),
        in_specs=[VMEM],
        out_specs=VMEM,
        scratch_shapes=incidence,
        compiler_params=params,
        cost_estimate=pl.CostEstimate(flops=1_000_000_000, bytes_accessed=1_000_000, transcendentals=0),
        name="own",
    )(packed)
    near_cells = pl.pallas_call(
        near_kernel,
        out_shape=jax.ShapeDtypeStruct((2 * LAYERS, 128, 128), f32),
        in_specs=[SMEM] + [VMEM] * 2,
        out_specs=VMEM,
        scratch_shapes=incidence,
        compiler_params=params,
        cost_estimate=pl.CostEstimate(flops=2_000_000_000, bytes_accessed=1_000_000, transcendentals=0),
        name="near",
    )(place, near_a, near_b)
    padded = (WINDOW + 1) * nodes - (nodes - 2 * (nodes // LAYERS))
    filtered = pl.pallas_call(
        filter_kernel,
        out_shape=jax.ShapeDtypeStruct((nodes, width), f32),
        in_specs=[SMEM] + [VMEM] * 8,
        out_specs=VMEM,
        scratch_shapes=[
            pltpu.VMEM((2 * LAYERS, 128, 128), f32),
            pltpu.VMEM((WINDOW * LAYERS // 2, 256, 256), bf16),
            pltpu.VMEM((padded, 2 * width), bf16),
            pltpu.VMEM((padded, 2 * width), bf16),
            pltpu.VMEM((WINDOW * nodes, width), f32),
            pltpu.VMEM((WINDOW * nodes, width), f32),
        ]
        + incidence,
        compiler_params=params,
        name="filter",
    )(place, packed, near_a, near_b, far_a, far_b, rank, own_cells, near_cells)

    all_states = lax.all_gather(filtered, "band", axis=1, tiled=True)
    term = pl.pallas_call(
        margin_kernel,
        out_shape=jax.ShapeDtypeStruct((state_order.shape[0], width), f32),
        in_specs=[SMEM, VMEM, VMEM],
        out_specs=VMEM,
        compiler_params=pltpu.CompilerParams(vmem_limit_bytes=40 * 2**20),
        name="margin",
    )(place, all_states, state_order[None, :])
    rows = state_order.shape[0] // doms
    parts = lax.all_to_all(term.reshape(doms, rows, width), "dom", 0, 0, tiled=True)
    return (filtered, parts.sum(0) * (1.0 / (nodes * doms)))


def solution(mesh):
    in_specs = (P("dom", "band"), P("dom"), P("dom"), P(None, "dom"), P("dom"), P())
    out_specs = (P("dom", "band"), P("dom", "band"))
    return jax.shard_map(shards, mesh=mesh, in_specs=in_specs, out_specs=out_specs, check_vma=False)
```

```python
import jax
import jax.numpy as jnp
import numpy as np
from jax import lax
from jax.experimental import pallas as pl
from jax.experimental.pallas import tpu as pltpu
from jax.sharding import PartitionSpec as P

DEGREE = 8
REACH = 2
WINDOW = 2 * REACH + 1
LAYERS = 4
EXTRA = 24

lower_cut = 1.5
upper_edge = 5.0
anchor_value = 0.4

half_span = (upper_edge - lower_cut) / 2.0
center = (upper_edge + lower_cut) / 2.0
sigma_first = half_span / (anchor_value - center)
gamma_value = 2.0 / sigma_first


VMEM = pl.BlockSpec(memory_space=pltpu.VMEM)
SMEM = pl.BlockSpec(memory_space=pltpu.SMEM)
ANY = pl.BlockSpec(memory_space=pl.ANY)
f32 = jnp.float32
bf16 = jnp.bfloat16


def dot(a, b):
    return lax.dot_general(a, b, (((1,), (0,)), ((), ())), preferred_element_type=f32)


def dot_t(a, b):
    return lax.dot_general(a, b, (((1,), (1,)), ((), ())), preferred_element_type=f32)


def split(x):
    high = x.astype(bf16)
    return high, (x - high.astype(f32)).astype(bf16)


def coarse_parts(x):
    parts = []
    for _ in range(3):
        scaled = x * float(2**19 + 1)
        part = scaled - (scaled - x)
        parts.append(part)
        x = x - part
    return parts


def exact(x):
    high, rest = x.astype(bf16), x
    terms = [high]
    for _ in range(2):
        rest = rest - terms[-1].astype(f32)
        terms.append(rest.astype(bf16))
    return terms


def cross(a, b):
    return lax.dot_general(a, b, (((0,), (0,)), ((), ())), preferred_element_type=f32)


def iota(shape, dim):
    return lax.broadcasted_iota(jnp.int32, shape, dim)


def flag(mask):
    return jnp.where(mask, 1.0, 0.0).astype(bf16)


def column_of(row):
    count = row.shape[1]
    terms = jnp.concatenate([t.astype(f32) for t in exact(row)] + [jnp.zeros((13, count), f32)], 0)
    return cross(terms.astype(bf16), jnp.ones((16, 128), bf16))


def sort_kernel(field, links, potential, mass, plane, out, rank_out, field_in, links_in, rows_in, plane_in, sems):
    nodes, width = field.shape
    copies = [
        pltpu.make_async_copy(field, field_in, sems.at[0]),
        pltpu.make_async_copy(links, links_in, sems.at[1]),
        pltpu.make_async_copy(potential, rows_in.at[pl.ds(0, 1)], sems.at[2]),
        pltpu.make_async_copy(mass, rows_in.at[pl.ds(1, 1)], sems.at[3]),
        pltpu.make_async_copy(plane, plane_in, sems.at[4]),
    ]
    for copy in copies:
        copy.start()
    for copy in copies[1:]:
        copy.wait()
    corners = links_in[...]
    corner_id = corners.astype(f32)
    plane_count = plane.shape[1]
    plane_row = jnp.concatenate([plane_in[...].astype(f32), jnp.full((1, 128 - plane_count), -1.0, f32)], 1)

    row_id = iota((nodes, nodes), 0).astype(f32)
    lane_id = iota((nodes, nodes), 1).astype(f32)
    row_small = row_id.astype(bf16)
    touched = None
    for a in range(8):
        hits = jnp.where(row_small == corner_id[a : a + 1, :].astype(bf16), jnp.ones_like(row_small), jnp.zeros_like(row_small))
        touched = hits if touched is None else touched + hits
    span = nodes // LAYERS
    by_layer = flag(iota((nodes, 128 * LAYERS), 0) // span == iota((nodes, 128 * LAYERS), 1) // 128)
    counts = dot(touched, by_layer)
    layer = [counts[:, 128 * i : 128 * (i + 1)] > 0.5 for i in range(LAYERS)]
    in_plane = flag(row_id[:, :128] == plane_row)
    is_plane = dot(in_plane, jnp.ones((128, 128), bf16)) > 0.5
    least = jnp.where(layer[0], 0.0, jnp.where(layer[1], 1.0, jnp.where(layer[2], 2.0, 3.0)))
    most = jnp.where(layer[3], 3.0, jnp.where(layer[2], 2.0, jnp.where(layer[1], 1.0, 0.0)))
    key = jnp.where(is_plane, -1.0, least + most)
    sub = iota((16, 128), 0)
    plane_facts = dot_t(
        jnp.where(sub == 0, 1.0, jnp.where(sub == 1, iota((16, 128), 1).astype(f32), 0.0)).astype(bf16), in_plane
    )
    row_counts = dot_t(flag(iota((16, nodes), 0) == iota((16, nodes), 1) // span), touched)
    row_layer = [row_counts[i : i + 1, :] > 0.5 for i in range(LAYERS)]
    row_least = jnp.where(row_layer[0], 0.0, jnp.where(row_layer[1], 1.0, jnp.where(row_layer[2], 2.0, 3.0)))
    row_most = jnp.where(row_layer[3], 3.0, jnp.where(row_layer[2], 2.0, jnp.where(row_layer[1], 1.0, 0.0)))
    key_row = jnp.where(plane_facts[0:1, :] > 0.5, -1.0, row_least + row_most)
    order_col = key * float(nodes) + row_id[:, :128]
    order_row = key_row * float(nodes) + lane_id[0:1, :]
    before = flag(jnp.concatenate([order_col] * (nodes // 128), 1) < order_row)
    counted = dot(jnp.ones((16, nodes), bf16), before)[0:1, :]
    rank = jnp.where(plane_facts[0:1, :] > 0.5, plane_facts[1:2, :], counted)
    rank_out[...] = jnp.broadcast_to(rank, rank_out.shape)

    low_lane = iota((8, 128), 1) < 64
    ranks = [jnp.broadcast_to(rank[:, 128 * h : 128 * (h + 1)], (8, 128)) for h in range(2)]
    for m in range(2):
        part = corners[:, 128 * m : 128 * (m + 1)]
        local = lax.bitwise_and(part, 127)
        found = [jnp.take_along_axis(r, local, axis=1) for r in ranks]
        place = jnp.where(part < 128, found[0], jnp.where(part < nodes, found[1], part.astype(f32)))
        place = place - jnp.where(low_lane, 128.0 * m, 128.0 * m + 64.0)
        turned = pltpu.roll(place, 64, 1)
        chance = rows_in[0:1, 128 * m : 128 * (m + 1)]
        chance = jnp.broadcast_to(chance, (8, 128))
        chance_turned = pltpu.roll(chance, 64, 1)
        for i in range(4):
            even, odd = slice(2 * i, 2 * i + 1), slice(2 * i + 1, 2 * i + 2)
            at = nodes + 8 * m + i
            out[at : at + 1, :] = jnp.where(low_lane[0:1], place[even], turned[odd])
            out[at + 4 : at + 5, :] = jnp.where(low_lane[0:1], turned[even], place[odd])
        at = nodes + 16 + 2 * m
        out[at : at + 1, :] = jnp.where(low_lane, chance, chance_turned)[0:1]
        out[at + 1 : at + 2, :] = jnp.where(low_lane, chance_turned, chance)[0:1]

    move = flag(row_id == rank)
    scale = lax.rsqrt(rows_in[1:2, :])
    terms = jnp.concatenate([t.astype(f32) for t in exact(scale)] + [jnp.zeros((13, nodes), f32)], 0)
    moved = dot_t(terms.astype(bf16), move)
    scale = moved[0:1] + moved[1:2] + moved[2:3]
    out[nodes + 20 : nodes + 21, :] = scale[:, :128]
    out[nodes + 21 : nodes + 22, :] = scale[:, 128:]
    out[nodes + 22 : nodes + 24, :] = jnp.zeros((2, 128), f32)
    copies[0].wait()
    sorted_field = dot(move, jnp.concatenate(exact(field_in[...]), 1))
    sorted_field = sorted_field[:, :width] + sorted_field[:, width : 2 * width] + sorted_field[:, 2 * width :]
    out[:nodes, :] = sorted_field * column_of(scale)


def layer_matrix(table, layer, scratch):
    plain, pair, third = scratch
    low_lane = iota((1, 128), 1) < 64
    chance = table[16 + layer : 17 + layer, :]
    stiff = (0.0, 1.0 / 2.0, 1.0 / 3.0, 1.0 / 6.0)
    mass = (1.0 / 8.0, 1.0 / 24.0, 1.0 / 72.0, 1.0 / 216.0)
    whole = [(0.5 * k + chance * m) * 0.125 for k, m in zip(stiff, mass)]

    def spread(row):
        return jnp.broadcast_to(row, (16, 128)).astype(bf16)

    weights = [
        [spread(part) for part in coarse_parts(jnp.where(low_lane, whole[j], whole[j + 1]))] for j in range(3)
    ]
    rows = table[4 * layer : 4 * layer + 4, :]
    turned = pltpu.roll(table[8 * (layer // 2) : 8 * (layer // 2) + 8, :], 64, 1)
    turned = turned[4 * (layer % 2) : 4 * (layer % 2) + 4, :]
    straight = [spread(rows[i : i + 1, :]) for i in range(4)]
    opposite = [spread(turned[i : i + 1, :]) for i in range(4)]
    sign = spread(jnp.where(low_lane, 1.0, -1.0))
    one, zero = jnp.ones((16, 128), bf16), jnp.zeros((16, 128), bf16)
    for r in range(8):
        local = (iota((16, 128), 0) + 16 * r).astype(f32).astype(bf16)
        items = [
            jnp.where(local == s, sign, zero) + jnp.where(local == o, one, zero) for s, o in zip(straight, opposite)
        ]
        for bit in (1, 2):
            mixed = [None] * 4
            for i in range(4):
                if not i & bit:
                    mixed[i] = items[i] + items[i | bit]
                    mixed[i | bit] = items[i] - items[i | bit]
            items = mixed
        for i in range(4):
            part = weights[bin(i).count("1")]
            lanes = slice(128 * i, 128 * (i + 1))
            plain[16 * r : 16 * r + 16, lanes] = items[i]
            pair[16 * r : 16 * r + 16, lanes] = items[i] * part[0]
            pair[128 + 16 * r : 128 + 16 * r + 16, lanes] = items[i] * part[1]
            third[16 * r : 16 * r + 16, lanes] = items[i] * part[2]
    both = dot_t(plain[...], pair[...])
    return both[:, :128] + both[:, 128:] + dot_t(plain[...], third[...])


def partition_matrices(table, scratch, layers, out, first):
    for layer in layers:
        out[first + layer] = layer_matrix(table, layer, [ref.at[layer] for ref in scratch])


def own_kernel(packed, rank, out, back, *scratch):
    nodes = back.shape[0]
    place = jnp.concatenate([column_of(rank[0:1, :])] * (nodes // 128), 1)
    back[...] = flag(place == iota((nodes, nodes), 1).astype(f32))
    partition_matrices(packed[packed.shape[0] - EXTRA :, :], scratch, range(LAYERS), out, 0)


def around(place, inner, outer, relay_a, relay_b):
    in_four = lax.rem(place[0], 4)
    is_even = lax.rem(place[0], 2) == 0
    left1 = jnp.where(is_even, outer, inner)
    right1 = jnp.where(is_even, inner, outer)
    left2 = jnp.where(in_four < 2, relay_b, relay_a)
    right2 = jnp.where(in_four < 2, relay_a, relay_b)
    return left2, left1, right1, right2


def outer_of(place, got_a, got_b, part):
    in_four = lax.rem(place[0], 4)
    by_b = jnp.logical_or(in_four == 0, in_four == 3)
    return jnp.where(by_b, got_b[part, :], got_a[part, :])


def near_kernel(place, inner, got_a, got_b, relay_a, out, *scratch):
    nodes = inner.shape[0] - EXTRA
    part = slice(nodes, nodes + EXTRA)
    for i, table in enumerate((inner[part, :], outer_of(place, got_a, got_b, part), relay_a[part, :])):
        partition_matrices(table, scratch, range(LAYERS), out, LAYERS * i)


def filter_kernel(place, packed, inner, got_a, got_b, relay_a, relay_b, back, own_cells, near_cells,
                  out, far_cells, bands, even, odd, field_a, field_b, *scratch):
    nodes, width = out.shape
    span = nodes // LAYERS
    table_part, field_part = slice(nodes, nodes + EXTRA), slice(0, nodes)
    last = relay_b[table_part, :]
    partition_matrices(last, scratch, range(LAYERS), far_cells, 0)

    def window(part):
        sides = around(place, inner[part, :], outer_of(place, got_a, got_b, part), relay_a[part, :], relay_b[part, :])
        return sides[:2] + (packed[part, :],) + sides[2:]

    tables = window(table_part)
    cells = []
    for i in range(LAYERS):
        cells.append(around(place, near_cells[i], near_cells[LAYERS + i], near_cells[2 * LAYERS + i], far_cells[i]))
    cells = [cells[i][0] for i in range(4)] + [cells[i][1] for i in range(4)] + [own_cells[i] for i in range(4)] + [
        cells[i][2] for i in range(4)] + [cells[i][3] for i in range(3)] + [None]

    low_lane = iota((128, 128), 1) < span
    on_first = iota((128, 128), 1) == iota((128, 128), 0) + span
    on_second = iota((128, 128), 1) == iota((128, 128), 0) - span
    blank = jnp.zeros((span, 128), f32)
    pairs = len(cells) // 2
    for q in range(WINDOW):
        scale = column_of(jnp.concatenate([tables[q][20:21], tables[q][21:22]], 1))
        weight = scale * scale * (1.0 / half_span)
        for j in (2 * q, 2 * q + 1):
            rows = slice(128 * (j - 2 * q), 128 * (j - 2 * q) + 128)
            turned = pltpu.roll(cells[2 * j], 64, 1)
            upper = blank if j == 0 else cells[2 * j - 1][span:, :]
            lower = blank if cells[2 * j + 1] is None else cells[2 * j + 1][:span, :]
            first = jnp.concatenate([upper, blank], 0) + jnp.where(low_lane, 0.0, turned)
            second = jnp.concatenate([blank, lower], 0) + jnp.where(low_lane, turned, 0.0)
            first = first * weight[rows, :] - jnp.where(on_first, center / half_span, 0.0)
            second = second * weight[rows, :] - jnp.where(on_second, center / half_span, 0.0)
            for lanes, value in ((slice(0, 128), first), (slice(128, 256), second)):
                high, low = split(value)
                bands[j, :128, lanes] = high
                bands[j, 128:, lanes] = low

    def put(target, at, value):
        count = value.shape[0]
        high, low = split(value)
        target[span + at : span + at + count, :width] = high
        target[span + at : span + at + count, width:] = low

    for target in (even, odd):
        target[:span, :] = jnp.zeros((span, 2 * width), bf16)
        target[span + WINDOW * nodes :, :] = jnp.zeros((span, 2 * width), bf16)
    for q, value in enumerate(window(field_part)):
        field_a[nodes * q : nodes * (q + 1), :] = value
        put(even, nodes * q, value)
    sigma_last = sigma_first
    final = []
    for k in range(1, DEGREE + 1):
        source, target = (even, odd) if k % 2 else (odd, even)
        newer = field_b if k % 2 else field_a
        if k == 1:
            gain, keep = sigma_first, None
        else:
            sigma_next = 1.0 / (gamma_value - sigma_last)
            gain, keep = 2.0 * sigma_next, sigma_last * sigma_next
            sigma_last = sigma_next
        for j in range(k // 2, pairs - k // 2):
            product = dot(bands[j], source[128 * j : 128 * j + 256, :])
            value = gain * (product[:128, :width] + (product[:128, width:] + product[128:, :width]))
            if keep is not None:
                value = value - keep * newer[128 * j : 128 * (j + 1), :]
            if k == DEGREE:
                final.append(value)
            else:
                newer[128 * j : 128 * (j + 1), :] = value
                put(target, 128 * j, value)
    scale = column_of(jnp.concatenate([tables[REACH][20:21], tables[REACH][21:22]], 1))
    moved = dot(back[...], jnp.concatenate(exact(jnp.concatenate(final, 0) / scale), 1))
    out[...] = moved[:, :width] + moved[:, width : 2 * width] + moved[:, 2 * width :]


def margin_kernel(place, states, order, out):
    band = place[1]
    count = order.shape[1]
    width = out.shape[1]
    state_id = lax.broadcasted_iota(jnp.int32, (count, count), 0)
    pick = jnp.where(state_id == order[...], 1.0, 0.0).astype(bf16)
    high, low = split(states[...])
    high = dot(high, pick)
    low = dot(low, pick).astype(bf16)
    high = high.astype(bf16)
    own_order = order[:, pl.ds(pl.multiple_of(band * width, width), width)]
    own_pick = jnp.where(state_id[:, :width] == own_order, 1.0, 0.0).astype(bf16)
    own_high, own_low = split(states[...])
    own_high = dot(own_high, own_pick).astype(bf16)
    own_low = dot(own_low, own_pick).astype(bf16)

    def cross(a, b):
        return lax.dot_general(a, b, (((0,), (0,)), ((), ())), preferred_element_type=f32)

    out[...] = cross(high, own_high) + cross(high, own_low) + cross(low, own_high)


def swapped(block, axis, pairs):
    count = lax.axis_size(axis)
    route = [
        step for a, b in pairs if 0 <= a and b < count for step in ((a, b), (b, a))
    ]
    return lax.ppermute(block, axis, route)


def shards(wavefunctions, node_mass, cell_potential, cell_nodes, plane_nodes, state_order):
    nodes, width = wavefunctions.shape
    doms = lax.axis_size("dom")
    place = jnp.stack([lax.axis_index("dom"), lax.axis_index("band")]).astype(jnp.int32)
    pairs = [(2 * i, 2 * i + 1) for i in range(doms)]
    fours = range(-1, doms // 4 + 1)
    mirror_a = [(4 * i + j, 4 * i + 3 - j) for i in fours for j in (0, 1)]
    mirror_b = [(4 * i + 2 + j, 4 * i + 5 - j) for i in fours for j in (0, 1)]
    params = pltpu.CompilerParams(vmem_limit_bytes=40 * 2**20)
    plane_count = plane_nodes.shape[0]

    packed, rank = pl.pallas_call(
        sort_kernel,
        out_shape=[jax.ShapeDtypeStruct((nodes + EXTRA, width), f32), jax.ShapeDtypeStruct((8, nodes), f32)],
        in_specs=[ANY] * 5,
        out_specs=[VMEM] * 2,
        scratch_shapes=[
            pltpu.VMEM((nodes, width), f32),
            pltpu.VMEM((8, nodes), jnp.int32),
            pltpu.VMEM((2, nodes), f32),
            pltpu.VMEM((1, plane_count), jnp.int32),
            pltpu.SemaphoreType.DMA((5,)),
        ],
        compiler_params=pltpu.CompilerParams(vmem_limit_bytes=60 * 2**20),
        name="sort",
    )(wavefunctions, cell_nodes, cell_potential[None, :], node_mass[None, :], plane_nodes[None, :])
    got_b, got_a, inner = [swapped(packed, "dom", route) for route in (mirror_b, mirror_a, pairs)]
    relay_a, relay_b = [swapped(block, "dom", pairs) for block in (got_a, got_b)]
    incidence = [
        pltpu.VMEM((LAYERS, 128, 512), bf16),
        pltpu.VMEM((LAYERS, 256, 512), bf16),
        pltpu.VMEM((LAYERS, 128, 512), bf16),
    ]
    own_cells, back = pl.pallas_call(
        own_kernel,
        out_shape=[jax.ShapeDtypeStruct((LAYERS, 128, 128), f32), jax.ShapeDtypeStruct((nodes, nodes), bf16)],
        in_specs=[VMEM] * 2,
        out_specs=[VMEM] * 2,
        scratch_shapes=incidence,
        compiler_params=params,
        cost_estimate=pl.CostEstimate(flops=1_000_000_000, bytes_accessed=1_000_000, transcendentals=0),
        name="own",
    )(packed, rank)
    near_cells = pl.pallas_call(
        near_kernel,
        out_shape=jax.ShapeDtypeStruct((3 * LAYERS, 128, 128), f32),
        in_specs=[SMEM] + [VMEM] * 4,
        out_specs=VMEM,
        scratch_shapes=incidence,
        compiler_params=params,
        cost_estimate=pl.CostEstimate(flops=2_000_000_000, bytes_accessed=1_000_000, transcendentals=0),
        name="near",
    )(place, inner, got_a, got_b, relay_a)
    padded = (WINDOW + 1) * nodes - (nodes - 2 * (nodes // LAYERS))
    filtered = pl.pallas_call(
        filter_kernel,
        out_shape=jax.ShapeDtypeStruct((nodes, width), f32),
        in_specs=[SMEM] + [VMEM] * 9,
        out_specs=VMEM,
        scratch_shapes=[
            pltpu.VMEM((LAYERS, 128, 128), f32),
            pltpu.VMEM((WINDOW * LAYERS // 2, 256, 256), bf16),
            pltpu.VMEM((padded, 2 * width), bf16),
            pltpu.VMEM((padded, 2 * width), bf16),
            pltpu.VMEM((WINDOW * nodes, width), f32),
            pltpu.VMEM((WINDOW * nodes, width), f32),
        ]
        + incidence,
        compiler_params=params,
        name="filter",
    )(place, packed, inner, got_a, got_b, relay_a, relay_b, back, own_cells, near_cells)

    all_states = lax.all_gather(filtered, "band", axis=1, tiled=True)
    term = pl.pallas_call(
        margin_kernel,
        out_shape=jax.ShapeDtypeStruct((state_order.shape[0], width), f32),
        in_specs=[SMEM, VMEM, VMEM],
        out_specs=VMEM,
        compiler_params=pltpu.CompilerParams(vmem_limit_bytes=40 * 2**20),
        name="margin",
    )(place, all_states, state_order[None, :])
    rows = state_order.shape[0] // doms
    parts = lax.all_to_all(term.reshape(doms, rows, width), "dom", 0, 0, tiled=True)
    return (filtered, parts.sum(0) * (1.0 / (nodes * doms)))


def solution(mesh):
    in_specs = (P("dom", "band"), P("dom"), P("dom"), P(None, "dom"), P("dom"), P())
    out_specs = (P("dom", "band"), P("dom", "band"))
    return jax.shard_map(shards, mesh=mesh, in_specs=in_specs, out_specs=out_specs, check_vma=False)
```

```python
import jax
import jax.numpy as jnp
import numpy as np
from jax import lax
from jax.experimental import pallas as pl
from jax.experimental.pallas import tpu as pltpu
from jax.sharding import PartitionSpec as P

DEGREE = 8
REACH = 2
WINDOW = 2 * REACH + 1
LAYERS = 4
EXTRA = 24

lower_cut = 1.5
upper_edge = 5.0
anchor_value = 0.4

half_span = (upper_edge - lower_cut) / 2.0
center = (upper_edge + lower_cut) / 2.0
sigma_first = half_span / (anchor_value - center)
gamma_value = 2.0 / sigma_first


VMEM = pl.BlockSpec(memory_space=pltpu.VMEM)
SMEM = pl.BlockSpec(memory_space=pltpu.SMEM)
ANY = pl.BlockSpec(memory_space=pl.ANY)
f32 = jnp.float32
bf16 = jnp.bfloat16


def dot(a, b):
    return lax.dot_general(a, b, (((1,), (0,)), ((), ())), preferred_element_type=f32)


def dot_t(a, b):
    return lax.dot_general(a, b, (((1,), (1,)), ((), ())), preferred_element_type=f32)


def split(x):
    high = x.astype(bf16)
    return high, (x - high.astype(f32)).astype(bf16)


def coarse_parts(x):
    parts = []
    for _ in range(3):
        scaled = x * float(2**19 + 1)
        part = scaled - (scaled - x)
        parts.append(part)
        x = x - part
    return parts


def exact(x):
    high, rest = x.astype(bf16), x
    terms = [high]
    for _ in range(2):
        rest = rest - terms[-1].astype(f32)
        terms.append(rest.astype(bf16))
    return terms


def cross(a, b):
    return lax.dot_general(a, b, (((0,), (0,)), ((), ())), preferred_element_type=f32)


def iota(shape, dim):
    return lax.broadcasted_iota(jnp.int32, shape, dim)


def flag(mask):
    return jnp.where(mask, 1.0, 0.0).astype(bf16)


def column_of(row):
    count = row.shape[1]
    terms = jnp.concatenate([t.astype(f32) for t in exact(row)] + [jnp.zeros((13, count), f32)], 0)
    return cross(terms.astype(bf16), jnp.ones((16, 128), bf16))


def sort_kernel(field, links, potential, mass, plane, out, rank_out, field_in, links_in, rows_in, plane_in, sems):
    nodes, width = field.shape
    copies = [
        pltpu.make_async_copy(field, field_in, sems.at[0]),
        pltpu.make_async_copy(links, links_in, sems.at[1]),
        pltpu.make_async_copy(potential, rows_in.at[pl.ds(0, 1)], sems.at[2]),
        pltpu.make_async_copy(mass, rows_in.at[pl.ds(1, 1)], sems.at[3]),
        pltpu.make_async_copy(plane, plane_in, sems.at[4]),
    ]
    for copy in copies:
        copy.start()
    for copy in copies[1:]:
        copy.wait()
    corners = links_in[...]
    corner_id = corners.astype(f32)
    plane_count = plane.shape[1]
    plane_row = jnp.concatenate([plane_in[...].astype(f32), jnp.full((1, 128 - plane_count), -1.0, f32)], 1)

    row_id = iota((nodes, nodes), 0).astype(f32)
    lane_id = iota((nodes, nodes), 1).astype(f32)
    row_small = row_id.astype(bf16)
    touched = None
    for a in range(8):
        hits = jnp.where(row_small == corner_id[a : a + 1, :].astype(bf16), jnp.ones_like(row_small), jnp.zeros_like(row_small))
        touched = hits if touched is None else touched + hits
    span = nodes // LAYERS
    by_layer = flag(iota((nodes, 128 * LAYERS), 0) // span == iota((nodes, 128 * LAYERS), 1) // 128)
    counts = dot(touched, by_layer)
    layer = [counts[:, 128 * i : 128 * (i + 1)] > 0.5 for i in range(LAYERS)]
    in_plane = flag(row_id[:, :128] == plane_row)
    is_plane = dot(in_plane, jnp.ones((128, 128), bf16)) > 0.5
    least = jnp.where(layer[0], 0.0, jnp.where(layer[1], 1.0, jnp.where(layer[2], 2.0, 3.0)))
    most = jnp.where(layer[3], 3.0, jnp.where(layer[2], 2.0, jnp.where(layer[1], 1.0, 0.0)))
    key = jnp.where(is_plane, -1.0, least + most)
    sub = iota((16, 128), 0)
    plane_facts = dot_t(
        jnp.where(sub == 0, 1.0, jnp.where(sub == 1, iota((16, 128), 1).astype(f32), 0.0)).astype(bf16), in_plane
    )
    row_counts = dot_t(flag(iota((16, nodes), 0) == iota((16, nodes), 1) // span), touched)
    row_layer = [row_counts[i : i + 1, :] > 0.5 for i in range(LAYERS)]
    row_least = jnp.where(row_layer[0], 0.0, jnp.where(row_layer[1], 1.0, jnp.where(row_layer[2], 2.0, 3.0)))
    row_most = jnp.where(row_layer[3], 3.0, jnp.where(row_layer[2], 2.0, jnp.where(row_layer[1], 1.0, 0.0)))
    key_row = jnp.where(plane_facts[0:1, :] > 0.5, -1.0, row_least + row_most)
    order_col = key * float(nodes) + row_id[:, :128]
    order_row = key_row * float(nodes) + lane_id[0:1, :]
    before = flag(jnp.concatenate([order_col] * (nodes // 128), 1) < order_row)
    counted = dot(jnp.ones((16, nodes), bf16), before)[0:1, :]
    rank = jnp.where(plane_facts[0:1, :] > 0.5, plane_facts[1:2, :], counted)
    rank_out[...] = jnp.broadcast_to(rank, rank_out.shape)

    low_lane = iota((8, 128), 1) < 64
    ranks = [jnp.broadcast_to(rank[:, 128 * h : 128 * (h + 1)], (8, 128)) for h in range(2)]
    for m in range(2):
        part = corners[:, 128 * m : 128 * (m + 1)]
        local = lax.bitwise_and(part, 127)
        found = [jnp.take_along_axis(r, local, axis=1) for r in ranks]
        place = jnp.where(part < 128, found[0], jnp.where(part < nodes, found[1], part.astype(f32)))
        place = place - jnp.where(low_lane, 128.0 * m, 128.0 * m + 64.0)
        turned = pltpu.roll(place, 64, 1)
        chance = rows_in[0:1, 128 * m : 128 * (m + 1)]
        chance = jnp.broadcast_to(chance, (8, 128))
        chance_turned = pltpu.roll(chance, 64, 1)
        for i in range(4):
            even, odd = slice(2 * i, 2 * i + 1), slice(2 * i + 1, 2 * i + 2)
            at = nodes + 8 * m + i
            out[at : at + 1, :] = jnp.where(low_lane[0:1], place[even], turned[odd])
            out[at + 4 : at + 5, :] = jnp.where(low_lane[0:1], turned[even], place[odd])
        at = nodes + 16 + 2 * m
        out[at : at + 1, :] = jnp.where(low_lane, chance, chance_turned)[0:1]
        out[at + 1 : at + 2, :] = jnp.where(low_lane, chance_turned, chance)[0:1]

    move = flag(row_id == rank)
    scale = lax.rsqrt(rows_in[1:2, :])
    terms = jnp.concatenate([t.astype(f32) for t in exact(scale)] + [jnp.zeros((13, nodes), f32)], 0)
    moved = dot_t(terms.astype(bf16), move)
    scale = moved[0:1] + moved[1:2] + moved[2:3]
    out[nodes + 20 : nodes + 21, :] = scale[:, :128]
    out[nodes + 21 : nodes + 22, :] = scale[:, 128:]
    out[nodes + 22 : nodes + 24, :] = jnp.zeros((2, 128), f32)
    copies[0].wait()
    sorted_field = dot(move, jnp.concatenate(exact(field_in[...]), 1))
    sorted_field = sorted_field[:, :width] + sorted_field[:, width : 2 * width] + sorted_field[:, 2 * width :]
    out[:nodes, :] = sorted_field * column_of(scale)


def layer_matrix(table, layer, scratch):
    plain, pair, third = scratch
    low_lane = iota((1, 128), 1) < 64
    chance = table[16 + layer : 17 + layer, :]
    stiff = (0.0, 1.0 / 2.0, 1.0 / 3.0, 1.0 / 6.0)
    mass = (1.0 / 8.0, 1.0 / 24.0, 1.0 / 72.0, 1.0 / 216.0)
    whole = [(0.5 * k + chance * m) * 0.125 for k, m in zip(stiff, mass)]

    def spread(row):
        return jnp.broadcast_to(row, (16, 128)).astype(bf16)

    weights = [
        [spread(part) for part in coarse_parts(jnp.where(low_lane, whole[j], whole[j + 1]))] for j in range(3)
    ]
    rows = table[4 * layer : 4 * layer + 4, :]
    turned = pltpu.roll(table[8 * (layer // 2) : 8 * (layer // 2) + 8, :], 64, 1)
    turned = turned[4 * (layer % 2) : 4 * (layer % 2) + 4, :]
    straight = [spread(rows[i : i + 1, :]) for i in range(4)]
    opposite = [spread(turned[i : i + 1, :]) for i in range(4)]
    sign = spread(jnp.where(low_lane, 1.0, -1.0))
    one, zero = jnp.ones((16, 128), bf16), jnp.zeros((16, 128), bf16)
    for r in range(8):
        local = (iota((16, 128), 0) + 16 * r).astype(f32).astype(bf16)
        items = [
            jnp.where(local == s, sign, zero) + jnp.where(local == o, one, zero) for s, o in zip(straight, opposite)
        ]
        for bit in (1, 2):
            mixed = [None] * 4
            for i in range(4):
                if not i & bit:
                    mixed[i] = items[i] + items[i | bit]
                    mixed[i | bit] = items[i] - items[i | bit]
            items = mixed
        for i in range(4):
            part = weights[bin(i).count("1")]
            lanes = slice(128 * i, 128 * (i + 1))
            plain[16 * r : 16 * r + 16, lanes] = items[i]
            pair[16 * r : 16 * r + 16, lanes] = items[i] * part[0]
            pair[128 + 16 * r : 128 + 16 * r + 16, lanes] = items[i] * part[1]
            third[16 * r : 16 * r + 16, lanes] = items[i] * part[2]
    both = dot_t(plain[...], pair[...])
    return both[:, :128] + both[:, 128:] + dot_t(plain[...], third[...])


def partition_matrices(table, scratch, layers, out, first):
    for layer in layers:
        out[first + layer] = layer_matrix(table, layer, [ref.at[layer] for ref in scratch])


def own_kernel(place, packed, rank, order, out, back, pick, own_pick, *scratch):
    nodes, (count, width) = back.shape[0], own_pick.shape
    state_id = iota((count, count), 0)
    pick[...] = flag(state_id == order[...])
    own_order = order[:, pl.ds(pl.multiple_of(place[1] * width, width), width)]
    own_pick[...] = flag(state_id[:, :width] == own_order)
    place = jnp.concatenate([column_of(rank[0:1, :])] * (nodes // 128), 1)
    back[...] = flag(place == iota((nodes, nodes), 1).astype(f32))
    partition_matrices(packed[packed.shape[0] - EXTRA :, :], scratch, range(LAYERS), out, 0)


def around(place, inner, outer, relay_a, relay_b):
    in_four = lax.rem(place[0], 4)
    is_even = lax.rem(place[0], 2) == 0
    left1 = jnp.where(is_even, outer, inner)
    right1 = jnp.where(is_even, inner, outer)
    left2 = jnp.where(in_four < 2, relay_b, relay_a)
    right2 = jnp.where(in_four < 2, relay_a, relay_b)
    return left2, left1, right1, right2


def outer_of(place, got_a, got_b, part):
    in_four = lax.rem(place[0], 4)
    by_b = jnp.logical_or(in_four == 0, in_four == 3)
    return jnp.where(by_b, got_b[part, :], got_a[part, :])


def near_kernel(place, inner, got_a, got_b, relay_a, out, *scratch):
    nodes = inner.shape[0] - EXTRA
    part = slice(nodes, nodes + EXTRA)
    for i, table in enumerate((inner[part, :], outer_of(place, got_a, got_b, part), relay_a[part, :])):
        partition_matrices(table, scratch, range(LAYERS), out, LAYERS * i)


def filter_kernel(place, packed, inner, got_a, got_b, relay_a, relay_b, own_cells, near_cells,
                  out, far_cells, bands, even, odd, field_a, field_b, *scratch):
    nodes, width = out.shape
    span = nodes // LAYERS
    table_part, field_part = slice(nodes, nodes + EXTRA), slice(0, nodes)
    last = relay_b[table_part, :]
    partition_matrices(last, scratch, range(LAYERS), far_cells, 0)

    def window(part):
        sides = around(place, inner[part, :], outer_of(place, got_a, got_b, part), relay_a[part, :], relay_b[part, :])
        return sides[:2] + (packed[part, :],) + sides[2:]

    tables = window(table_part)
    cells = []
    for i in range(LAYERS):
        cells.append(around(place, near_cells[i], near_cells[LAYERS + i], near_cells[2 * LAYERS + i], far_cells[i]))
    cells = [cells[i][0] for i in range(4)] + [cells[i][1] for i in range(4)] + [own_cells[i] for i in range(4)] + [
        cells[i][2] for i in range(4)] + [cells[i][3] for i in range(3)] + [None]

    low_lane = iota((128, 128), 1) < span
    on_first = iota((128, 128), 1) == iota((128, 128), 0) + span
    on_second = iota((128, 128), 1) == iota((128, 128), 0) - span
    blank = jnp.zeros((span, 128), f32)
    pairs = len(cells) // 2
    for q in range(WINDOW):
        scale = column_of(jnp.concatenate([tables[q][20:21], tables[q][21:22]], 1))
        weight = scale * scale * (1.0 / half_span)
        for j in (2 * q, 2 * q + 1):
            rows = slice(128 * (j - 2 * q), 128 * (j - 2 * q) + 128)
            turned = pltpu.roll(cells[2 * j], 64, 1)
            upper = blank if j == 0 else cells[2 * j - 1][span:, :]
            lower = blank if cells[2 * j + 1] is None else cells[2 * j + 1][:span, :]
            first = jnp.concatenate([upper, blank], 0) + jnp.where(low_lane, 0.0, turned)
            second = jnp.concatenate([blank, lower], 0) + jnp.where(low_lane, turned, 0.0)
            first = first * weight[rows, :] - jnp.where(on_first, center / half_span, 0.0)
            second = second * weight[rows, :] - jnp.where(on_second, center / half_span, 0.0)
            for lanes, value in ((slice(0, 128), first), (slice(128, 256), second)):
                high, low = split(value)
                bands[j, :128, lanes] = high
                bands[j, 128:, lanes] = low

    def put(target, at, value):
        count = value.shape[0]
        high, low = split(value)
        target[span + at : span + at + count, :width] = high
        target[span + at : span + at + count, width:] = low

    for target in (even, odd):
        target[:span, :] = jnp.zeros((span, 2 * width), bf16)
        target[span + WINDOW * nodes :, :] = jnp.zeros((span, 2 * width), bf16)
    for q, value in enumerate(window(field_part)):
        field_a[nodes * q : nodes * (q + 1), :] = value
        put(even, nodes * q, value)
    sigma_last = sigma_first
    final = []
    for k in range(1, DEGREE + 1):
        source, target = (even, odd) if k % 2 else (odd, even)
        newer = field_b if k % 2 else field_a
        if k == 1:
            gain, keep = sigma_first, None
        else:
            sigma_next = 1.0 / (gamma_value - sigma_last)
            gain, keep = 2.0 * sigma_next, sigma_last * sigma_next
            sigma_last = sigma_next
        for j in range(k // 2, pairs - k // 2):
            product = dot(bands[j], source[128 * j : 128 * j + 256, :])
            value = gain * (product[:128, :width] + (product[:128, width:] + product[128:, :width]))
            if keep is not None:
                value = value - keep * newer[128 * j : 128 * (j + 1), :]
            if k == DEGREE:
                final.append(value)
            else:
                newer[128 * j : 128 * (j + 1), :] = value
                put(target, 128 * j, value)
    scale = column_of(jnp.concatenate([tables[REACH][20:21], tables[REACH][21:22]], 1))
    out[...] = jnp.concatenate(final, 0) / scale


def margin_kernel(states, pick, own_pick, own, back, out, filtered, original, sem):
    width = out.shape[1]
    moved = dot(back[...], jnp.concatenate(exact(own[...]), 1))
    original[...] = moved[:, :width] + moved[:, width : 2 * width] + moved[:, 2 * width :]
    copy = pltpu.make_async_copy(original, filtered, sem)
    copy.start()
    high, low = split(states[...])
    own_high = dot(high, own_pick[...]).astype(bf16)
    own_low = dot(low, own_pick[...]).astype(bf16)
    part = cross(own_high, high) + cross(own_high, low) + cross(own_low, high)
    chosen = [dot(term, pick[...]) for term in exact(part)]
    out[...] = (chosen[0] + chosen[1] + chosen[2]).T
    copy.wait()


def swapped(block, axis, pairs):
    count = lax.axis_size(axis)
    route = [
        step for a, b in pairs if 0 <= a and b < count for step in ((a, b), (b, a))
    ]
    return lax.ppermute(block, axis, route)


def shards(wavefunctions, node_mass, cell_potential, cell_nodes, plane_nodes, state_order):
    nodes, width = wavefunctions.shape
    doms = lax.axis_size("dom")
    place = jnp.stack([lax.axis_index("dom"), lax.axis_index("band")]).astype(jnp.int32)
    pairs = [(2 * i, 2 * i + 1) for i in range(doms)]
    fours = range(-1, doms // 4 + 1)
    mirror_a = [(4 * i + j, 4 * i + 3 - j) for i in fours for j in (0, 1)]
    mirror_b = [(4 * i + 2 + j, 4 * i + 5 - j) for i in fours for j in (0, 1)]
    params = pltpu.CompilerParams(vmem_limit_bytes=40 * 2**20)
    plane_count = plane_nodes.shape[0]

    packed, rank = pl.pallas_call(
        sort_kernel,
        out_shape=[jax.ShapeDtypeStruct((nodes + EXTRA, width), f32), jax.ShapeDtypeStruct((8, nodes), f32)],
        in_specs=[ANY] * 5,
        out_specs=[VMEM] * 2,
        scratch_shapes=[
            pltpu.VMEM((nodes, width), f32),
            pltpu.VMEM((8, nodes), jnp.int32),
            pltpu.VMEM((2, nodes), f32),
            pltpu.VMEM((1, plane_count), jnp.int32),
            pltpu.SemaphoreType.DMA((5,)),
        ],
        compiler_params=pltpu.CompilerParams(vmem_limit_bytes=60 * 2**20),
        name="sort",
    )(wavefunctions, cell_nodes, cell_potential[None, :], node_mass[None, :], plane_nodes[None, :])
    got_b, got_a, inner = [swapped(packed, "dom", route) for route in (mirror_b, mirror_a, pairs)]
    relay_a, relay_b = [swapped(block, "dom", pairs) for block in (got_a, got_b)]
    incidence = [
        pltpu.VMEM((LAYERS, 128, 512), bf16),
        pltpu.VMEM((LAYERS, 256, 512), bf16),
        pltpu.VMEM((LAYERS, 128, 512), bf16),
    ]
    states = state_order.shape[0]
    own_cells, back, pick, own_pick = pl.pallas_call(
        own_kernel,
        out_shape=[
            jax.ShapeDtypeStruct((LAYERS, 128, 128), f32),
            jax.ShapeDtypeStruct((nodes, nodes), bf16),
            jax.ShapeDtypeStruct((states, states), bf16),
            jax.ShapeDtypeStruct((states, width), bf16),
        ],
        in_specs=[SMEM] + [VMEM] * 3,
        out_specs=[VMEM] * 4,
        scratch_shapes=incidence,
        compiler_params=params,
        cost_estimate=pl.CostEstimate(flops=1_000_000_000, bytes_accessed=1_000_000, transcendentals=0),
        name="own",
    )(place, packed, rank, state_order[None, :])
    near_cells = pl.pallas_call(
        near_kernel,
        out_shape=jax.ShapeDtypeStruct((3 * LAYERS, 128, 128), f32),
        in_specs=[SMEM] + [VMEM] * 4,
        out_specs=VMEM,
        scratch_shapes=incidence,
        compiler_params=params,
        cost_estimate=pl.CostEstimate(flops=2_000_000_000, bytes_accessed=1_000_000, transcendentals=0),
        name="near",
    )(place, inner, got_a, got_b, relay_a)
    padded = (WINDOW + 1) * nodes - (nodes - 2 * (nodes // LAYERS))
    by_layer = pl.pallas_call(
        filter_kernel,
        out_shape=jax.ShapeDtypeStruct((nodes, width), f32),
        in_specs=[SMEM] + [VMEM] * 8,
        out_specs=VMEM,
        scratch_shapes=[
            pltpu.VMEM((LAYERS, 128, 128), f32),
            pltpu.VMEM((WINDOW * LAYERS // 2, 256, 256), bf16),
            pltpu.VMEM((padded, 2 * width), bf16),
            pltpu.VMEM((padded, 2 * width), bf16),
            pltpu.VMEM((WINDOW * nodes, width), f32),
            pltpu.VMEM((WINDOW * nodes, width), f32),
        ]
        + incidence,
        compiler_params=params,
        name="filter",
    )(place, packed, inner, got_a, got_b, relay_a, relay_b, own_cells, near_cells)

    all_states = lax.all_gather(by_layer, "band", axis=1, tiled=True)
    term, filtered = pl.pallas_call(
        margin_kernel,
        out_shape=[jax.ShapeDtypeStruct((states, width), f32), jax.ShapeDtypeStruct((nodes, width), f32)],
        in_specs=[VMEM] * 5,
        out_specs=[VMEM, ANY],
        scratch_shapes=[pltpu.VMEM((nodes, width), f32), pltpu.SemaphoreType.DMA],
        compiler_params=params,
        name="margin",
    )(all_states, pick, own_pick, by_layer, back)
    rows = state_order.shape[0] // doms
    parts = lax.all_to_all(term.reshape(doms, rows, width), "dom", 0, 0, tiled=True)
    return (filtered, parts.sum(0) * (1.0 / (nodes * doms)))


def solution(mesh):
    in_specs = (P("dom", "band"), P("dom"), P("dom"), P(None, "dom"), P("dom"), P())
    out_specs = (P("dom", "band"), P("dom", "band"))
    return jax.shard_map(shards, mesh=mesh, in_specs=in_specs, out_specs=out_specs, check_vma=False)
```

```python
import jax
import jax.numpy as jnp
import numpy as np
from jax import lax
from jax.experimental import pallas as pl
from jax.experimental.pallas import tpu as pltpu
from jax.sharding import PartitionSpec as P

DEGREE = 8
REACH = 2
WINDOW = 2 * REACH + 1
LAYERS = 4
EXTRA = 24

lower_cut = 1.5
upper_edge = 5.0
anchor_value = 0.4

half_span = (upper_edge - lower_cut) / 2.0
center = (upper_edge + lower_cut) / 2.0
sigma_first = half_span / (anchor_value - center)
gamma_value = 2.0 / sigma_first


VMEM = pl.BlockSpec(memory_space=pltpu.VMEM)
SMEM = pl.BlockSpec(memory_space=pltpu.SMEM)
ANY = pl.BlockSpec(memory_space=pl.ANY)
f32 = jnp.float32
bf16 = jnp.bfloat16


def final_gain():
    sigma = gain = sigma_first
    for _ in range(DEGREE - 1):
        sigma = 1.0 / (gamma_value - sigma)
        gain = gain * 2.0 * sigma
    return gain


def dot(a, b):
    return lax.dot_general(a, b, (((1,), (0,)), ((), ())), preferred_element_type=f32)


def dot_t(a, b):
    return lax.dot_general(a, b, (((1,), (1,)), ((), ())), preferred_element_type=f32)


def split(x):
    high = x.astype(bf16)
    return high, (x - high.astype(f32)).astype(bf16)


def coarse_parts(x):
    parts = []
    for _ in range(3):
        scaled = x * float(2**19 + 1)
        part = scaled - (scaled - x)
        parts.append(part)
        x = x - part
    return parts


def exact(x):
    high, rest = x.astype(bf16), x
    terms = [high]
    for _ in range(2):
        rest = rest - terms[-1].astype(f32)
        terms.append(rest.astype(bf16))
    return terms


def cross(a, b):
    return lax.dot_general(a, b, (((0,), (0,)), ((), ())), preferred_element_type=f32)


def iota(shape, dim):
    return lax.broadcasted_iota(jnp.int32, shape, dim)


def flag(mask):
    return jnp.where(mask, 1.0, 0.0).astype(bf16)


def column_of(row):
    count = row.shape[1]
    terms = jnp.concatenate([t.astype(f32) for t in exact(row)] + [jnp.zeros((13, count), f32)], 0)
    return cross(terms.astype(bf16), jnp.ones((16, 128), bf16))


def sort_kernel(field, links, potential, mass, plane, out, rank_out, field_in, links_in, rows_in, plane_in, sems):
    nodes, width = field.shape
    copies = [
        pltpu.make_async_copy(field, field_in, sems.at[0]),
        pltpu.make_async_copy(links, links_in, sems.at[1]),
        pltpu.make_async_copy(potential, rows_in.at[pl.ds(0, 1)], sems.at[2]),
        pltpu.make_async_copy(mass, rows_in.at[pl.ds(1, 1)], sems.at[3]),
        pltpu.make_async_copy(plane, plane_in, sems.at[4]),
    ]
    for copy in copies:
        copy.start()
    for copy in copies[1:]:
        copy.wait()
    corners = links_in[...]
    corner_id = corners.astype(f32)
    plane_count = plane.shape[1]
    plane_row = jnp.concatenate([plane_in[...].astype(f32), jnp.full((1, 128 - plane_count), -1.0, f32)], 1)

    scale = lax.rsqrt(rows_in[1:2, :])
    copies[0].wait()
    field_terms = jnp.concatenate(exact(field_in[...] * column_of(scale)), 1)

    row_id = iota((nodes, nodes), 0).astype(f32)
    lane_id = iota((nodes, nodes), 1).astype(f32)
    row_small = row_id.astype(bf16)
    touched = None
    for a in range(8):
        hits = jnp.where(row_small == corner_id[a : a + 1, :].astype(bf16), jnp.ones_like(row_small), jnp.zeros_like(row_small))
        touched = hits if touched is None else touched + hits
    span = nodes // LAYERS
    by_layer = flag(iota((nodes, 128 * LAYERS), 0) // span == iota((nodes, 128 * LAYERS), 1) // 128)
    counts = dot(touched, by_layer)
    layer = [counts[:, 128 * i : 128 * (i + 1)] > 0.5 for i in range(LAYERS)]
    in_plane = flag(row_id[:, :128] == plane_row)
    is_plane = dot(in_plane, jnp.ones((128, 128), bf16)) > 0.5
    least = jnp.where(layer[0], 0.0, jnp.where(layer[1], 1.0, jnp.where(layer[2], 2.0, 3.0)))
    most = jnp.where(layer[3], 3.0, jnp.where(layer[2], 2.0, jnp.where(layer[1], 1.0, 0.0)))
    key = jnp.where(is_plane, -1.0, least + most)
    sub = iota((16, 128), 0)
    plane_facts = dot_t(
        jnp.where(sub == 0, 1.0, jnp.where(sub == 1, iota((16, 128), 1).astype(f32), 0.0)).astype(bf16), in_plane
    )
    row_counts = dot_t(flag(iota((16, nodes), 0) == iota((16, nodes), 1) // span), touched)
    row_layer = [row_counts[i : i + 1, :] > 0.5 for i in range(LAYERS)]
    row_least = jnp.where(row_layer[0], 0.0, jnp.where(row_layer[1], 1.0, jnp.where(row_layer[2], 2.0, 3.0)))
    row_most = jnp.where(row_layer[3], 3.0, jnp.where(row_layer[2], 2.0, jnp.where(row_layer[1], 1.0, 0.0)))
    key_row = jnp.where(plane_facts[0:1, :] > 0.5, -1.0, row_least + row_most)
    order_col = key * float(nodes) + row_id[:, :128]
    order_row = key_row * float(nodes) + lane_id[0:1, :]
    before = flag(jnp.concatenate([order_col] * (nodes // 128), 1) < order_row)
    counted = dot(jnp.ones((16, nodes), bf16), before)[0:1, :]
    rank = jnp.where(plane_facts[0:1, :] > 0.5, plane_facts[1:2, :], counted)
    rank_out[...] = jnp.broadcast_to(rank, rank_out.shape)

    low_lane = iota((8, 128), 1) < 64
    ranks = [jnp.broadcast_to(rank[:, 128 * h : 128 * (h + 1)], (8, 128)) for h in range(2)]
    for m in range(2):
        part = corners[:, 128 * m : 128 * (m + 1)]
        local = lax.bitwise_and(part, 127)
        found = [jnp.take_along_axis(r, local, axis=1) for r in ranks]
        place = jnp.where(part < 128, found[0], jnp.where(part < nodes, found[1], part.astype(f32)))
        place = place - jnp.where(low_lane, 128.0 * m, 128.0 * m + 64.0)
        turned = pltpu.roll(place, 64, 1)
        chance = rows_in[0:1, 128 * m : 128 * (m + 1)]
        chance = jnp.broadcast_to(chance, (8, 128))
        chance_turned = pltpu.roll(chance, 64, 1)
        for i in range(4):
            even, odd = slice(2 * i, 2 * i + 1), slice(2 * i + 1, 2 * i + 2)
            at = nodes + 8 * m + i
            out[at : at + 1, :] = jnp.where(low_lane[0:1], place[even], turned[odd])
            out[at + 4 : at + 5, :] = jnp.where(low_lane[0:1], turned[even], place[odd])
        at = nodes + 16 + 2 * m
        out[at : at + 1, :] = jnp.where(low_lane, chance, chance_turned)[0:1]
        out[at + 1 : at + 2, :] = jnp.where(low_lane, chance_turned, chance)[0:1]

    move = flag(row_id == rank)
    terms = jnp.concatenate([t.astype(f32) for t in exact(scale)] + [jnp.zeros((13, nodes), f32)], 0)
    moved = dot_t(terms.astype(bf16), move)
    scale = moved[0:1] + moved[1:2] + moved[2:3]
    out[nodes + 20 : nodes + 21, :] = scale[:, :128]
    out[nodes + 21 : nodes + 22, :] = scale[:, 128:]
    out[nodes + 22 : nodes + 24, :] = jnp.zeros((2, 128), f32)
    sorted_field = dot(move, field_terms)
    out[:nodes, :] = sorted_field[:, :width] + sorted_field[:, width : 2 * width] + sorted_field[:, 2 * width :]


def layer_matrix(table, layer, scratch):
    plain, pair, third = scratch
    low_lane = iota((1, 128), 1) < 64
    chance = table[16 + layer : 17 + layer, :]
    stiff = (0.0, 1.0 / 2.0, 1.0 / 3.0, 1.0 / 6.0)
    mass = (1.0 / 8.0, 1.0 / 24.0, 1.0 / 72.0, 1.0 / 216.0)
    whole = [(0.5 * k + chance * m) * 0.125 for k, m in zip(stiff, mass)]

    def spread(row):
        return jnp.broadcast_to(row, (16, 128)).astype(bf16)

    weights = [
        [spread(part) for part in coarse_parts(jnp.where(low_lane, whole[j], whole[j + 1]))] for j in range(3)
    ]
    rows = table[4 * layer : 4 * layer + 4, :]
    turned = pltpu.roll(table[8 * (layer // 2) : 8 * (layer // 2) + 8, :], 64, 1)
    turned = turned[4 * (layer % 2) : 4 * (layer % 2) + 4, :]
    straight = [spread(rows[i : i + 1, :]) for i in range(4)]
    opposite = [spread(turned[i : i + 1, :]) for i in range(4)]
    sign = spread(jnp.where(low_lane, 1.0, -1.0))
    one, zero = jnp.ones((16, 128), bf16), jnp.zeros((16, 128), bf16)
    for r in range(8):
        local = (iota((16, 128), 0) + 16 * r).astype(f32).astype(bf16)
        items = [
            jnp.where(local == s, sign, zero) + jnp.where(local == o, one, zero) for s, o in zip(straight, opposite)
        ]
        for bit in (1, 2):
            mixed = [None] * 4
            for i in range(4):
                if not i & bit:
                    mixed[i] = items[i] + items[i | bit]
                    mixed[i | bit] = items[i] - items[i | bit]
            items = mixed
        for i in range(4):
            part = weights[bin(i).count("1")]
            lanes = slice(128 * i, 128 * (i + 1))
            plain[16 * r : 16 * r + 16, lanes] = items[i]
            pair[16 * r : 16 * r + 16, lanes] = items[i] * part[0]
            pair[128 + 16 * r : 128 + 16 * r + 16, lanes] = items[i] * part[1]
            third[16 * r : 16 * r + 16, lanes] = items[i] * part[2]
    both = dot_t(plain[...], pair[...])
    return both[:, :128] + both[:, 128:] + dot_t(plain[...], third[...])


def partition_matrices(table, scratch, layers, out, first):
    for layer in layers:
        out[first + layer] = layer_matrix(table, layer, [ref.at[layer] for ref in scratch])


def own_kernel(place, packed, rank, order, out, back, pick, own_pick, *scratch):
    nodes, (count, width) = back.shape[0], own_pick.shape
    state_id = iota((count, count), 0)
    pick[...] = flag(state_id == order[...])
    own_order = order[:, pl.ds(pl.multiple_of(place[1] * width, width), width)]
    own_pick[...] = flag(state_id[:, :width] == own_order)
    place = jnp.concatenate([column_of(rank[0:1, :])] * (nodes // 128), 1)
    back[...] = flag(place == iota((nodes, nodes), 1).astype(f32))
    partition_matrices(packed[packed.shape[0] - EXTRA :, :], scratch, range(LAYERS), out, 0)


def around(place, inner, outer, relay_a, relay_b):
    in_four = lax.rem(place[0], 4)
    is_even = lax.rem(place[0], 2) == 0
    left1 = jnp.where(is_even, outer, inner)
    right1 = jnp.where(is_even, inner, outer)
    left2 = jnp.where(in_four < 2, relay_b, relay_a)
    right2 = jnp.where(in_four < 2, relay_a, relay_b)
    return left2, left1, right1, right2


def outer_of(place, got_a, got_b, part):
    in_four = lax.rem(place[0], 4)
    by_b = jnp.logical_or(in_four == 0, in_four == 3)
    return jnp.where(by_b, got_b[part, :], got_a[part, :])


def near_kernel(place, inner, got_a, got_b, relay_a, out, *scratch):
    nodes = inner.shape[0] - EXTRA
    part = slice(nodes, nodes + EXTRA)
    for i, table in enumerate((inner[part, :], outer_of(place, got_a, got_b, part), relay_a[part, :])):
        partition_matrices(table, scratch, range(LAYERS), out, LAYERS * i)


def filter_kernel(place, packed, inner, got_a, got_b, relay_a, relay_b, own_cells, near_cells,
                  out, far_cells, bands, even, odd, field_a, field_b, *scratch):
    nodes, width = out.shape
    span = nodes // LAYERS
    table_part, field_part = slice(nodes, nodes + EXTRA), slice(0, nodes)
    last = relay_b[table_part, :]
    partition_matrices(last, scratch, range(LAYERS), far_cells, 0)

    def window(part):
        sides = around(place, inner[part, :], outer_of(place, got_a, got_b, part), relay_a[part, :], relay_b[part, :])
        return sides[:2] + (packed[part, :],) + sides[2:]

    tables = window(table_part)
    cells = []
    for i in range(LAYERS):
        cells.append(around(place, near_cells[i], near_cells[LAYERS + i], near_cells[2 * LAYERS + i], far_cells[i]))
    cells = [cells[i][0] for i in range(4)] + [cells[i][1] for i in range(4)] + [own_cells[i] for i in range(4)] + [
        cells[i][2] for i in range(4)] + [cells[i][3] for i in range(3)] + [None]

    low_lane = iota((128, 128), 1) < span
    on_first = iota((128, 128), 1) == iota((128, 128), 0) + span
    on_second = iota((128, 128), 1) == iota((128, 128), 0) - span
    blank = jnp.zeros((span, 128), f32)
    pairs = len(cells) // 2
    for q in range(WINDOW):
        scale = column_of(jnp.concatenate([tables[q][20:21], tables[q][21:22]], 1))
        weight = scale * scale * (1.0 / half_span)
        for j in (2 * q, 2 * q + 1):
            rows = slice(128 * (j - 2 * q), 128 * (j - 2 * q) + 128)
            turned = pltpu.roll(cells[2 * j], 64, 1)
            upper = blank if j == 0 else cells[2 * j - 1][span:, :]
            lower = blank if cells[2 * j + 1] is None else cells[2 * j + 1][:span, :]
            first = jnp.concatenate([upper, blank], 0) + jnp.where(low_lane, 0.0, turned)
            second = jnp.concatenate([blank, lower], 0) + jnp.where(low_lane, turned, 0.0)
            first = first * weight[rows, :] - jnp.where(on_first, center / half_span, 0.0)
            second = second * weight[rows, :] - jnp.where(on_second, center / half_span, 0.0)
            for lanes, value in ((slice(0, 128), first), (slice(128, 256), second)):
                high, low = split(value)
                bands[j, :128, lanes] = high
                bands[j, 128:, lanes] = low

    def put(target, at, value):
        count = value.shape[0]
        high, low = split(value)
        target[span + at : span + at + count, :width] = high
        target[span + at : span + at + count, width:] = low

    for target in (even, odd):
        target[:span, :] = jnp.zeros((span, 2 * width), bf16)
        target[span + WINDOW * nodes :, :] = jnp.zeros((span, 2 * width), bf16)
    for q, value in enumerate(window(field_part)):
        field_a[nodes * q : nodes * (q + 1), :] = value
        put(even, nodes * q, value)
    final = []
    for k in range(1, DEGREE + 1):
        source, target = (even, odd) if k % 2 else (odd, even)
        newer = field_b if k % 2 else field_a
        keep = {1: None, 2: 0.5}.get(k, 0.25)
        for j in range(k // 2, pairs - k // 2):
            product = dot(bands[j], source[128 * j : 128 * j + 256, :])
            value = product[:128, :width] + (product[:128, width:] + product[128:, :width])
            if keep is not None:
                value = value - keep * newer[128 * j : 128 * (j + 1), :]
            if k == DEGREE:
                final.append(value)
            else:
                newer[128 * j : 128 * (j + 1), :] = value
                put(target, 128 * j, value)
    out[...] = jnp.concatenate(final, 0) * (final_gain() / column_of(
        jnp.concatenate([tables[REACH][20:21], tables[REACH][21:22]], 1)))


def margin_kernel(states, pick, own_pick, own, back, out, filtered, original, sem):
    width = out.shape[1]
    moved = dot(back[...], jnp.concatenate(exact(own[...]), 1))
    original[...] = moved[:, :width] + moved[:, width : 2 * width] + moved[:, 2 * width :]
    copy = pltpu.make_async_copy(original, filtered, sem)
    copy.start()
    high, low = split(states[...])
    own_high = dot(high, own_pick[...]).astype(bf16)
    own_low = dot(low, own_pick[...]).astype(bf16)
    part = cross(own_high, high) + cross(own_high, low) + cross(own_low, high)
    chosen = [dot(term, pick[...]) for term in exact(part)]
    out[...] = (chosen[0] + chosen[1] + chosen[2]).T
    copy.wait()


def swapped(block, axis, pairs):
    count = lax.axis_size(axis)
    route = [
        step for a, b in pairs if 0 <= a and b < count for step in ((a, b), (b, a))
    ]
    return lax.ppermute(block, axis, route)


def shards(wavefunctions, node_mass, cell_potential, cell_nodes, plane_nodes, state_order):
    nodes, width = wavefunctions.shape
    doms = lax.axis_size("dom")
    place = jnp.stack([lax.axis_index("dom"), lax.axis_index("band")]).astype(jnp.int32)
    pairs = [(2 * i, 2 * i + 1) for i in range(doms)]
    fours = range(-1, doms // 4 + 1)
    mirror_a = [(4 * i + j, 4 * i + 3 - j) for i in fours for j in (0, 1)]
    mirror_b = [(4 * i + 2 + j, 4 * i + 5 - j) for i in fours for j in (0, 1)]
    params = pltpu.CompilerParams(vmem_limit_bytes=40 * 2**20)
    plane_count = plane_nodes.shape[0]

    packed, rank = pl.pallas_call(
        sort_kernel,
        out_shape=[jax.ShapeDtypeStruct((nodes + EXTRA, width), f32), jax.ShapeDtypeStruct((8, nodes), f32)],
        in_specs=[ANY] * 5,
        out_specs=[VMEM] * 2,
        scratch_shapes=[
            pltpu.VMEM((nodes, width), f32),
            pltpu.VMEM((8, nodes), jnp.int32),
            pltpu.VMEM((2, nodes), f32),
            pltpu.VMEM((1, plane_count), jnp.int32),
            pltpu.SemaphoreType.DMA((5,)),
        ],
        compiler_params=pltpu.CompilerParams(vmem_limit_bytes=60 * 2**20),
        name="sort",
    )(wavefunctions, cell_nodes, cell_potential[None, :], node_mass[None, :], plane_nodes[None, :])
    got_b, got_a, inner = [swapped(packed, "dom", route) for route in (mirror_b, mirror_a, pairs)]
    relay_a, relay_b = [swapped(block, "dom", pairs) for block in (got_a, got_b)]
    incidence = [
        pltpu.VMEM((LAYERS, 128, 512), bf16),
        pltpu.VMEM((LAYERS, 256, 512), bf16),
        pltpu.VMEM((LAYERS, 128, 512), bf16),
    ]
    states = state_order.shape[0]
    own_cells, back, pick, own_pick = pl.pallas_call(
        own_kernel,
        out_shape=[
            jax.ShapeDtypeStruct((LAYERS, 128, 128), f32),
            jax.ShapeDtypeStruct((nodes, nodes), bf16),
            jax.ShapeDtypeStruct((states, states), bf16),
            jax.ShapeDtypeStruct((states, width), bf16),
        ],
        in_specs=[SMEM] + [VMEM] * 3,
        out_specs=[VMEM] * 4,
        scratch_shapes=incidence,
        compiler_params=params,
        cost_estimate=pl.CostEstimate(flops=1_000_000_000, bytes_accessed=1_000_000, transcendentals=0),
        name="own",
    )(place, packed, rank, state_order[None, :])
    near_cells = pl.pallas_call(
        near_kernel,
        out_shape=jax.ShapeDtypeStruct((3 * LAYERS, 128, 128), f32),
        in_specs=[SMEM] + [VMEM] * 4,
        out_specs=VMEM,
        scratch_shapes=incidence,
        compiler_params=params,
        cost_estimate=pl.CostEstimate(flops=2_000_000_000, bytes_accessed=1_000_000, transcendentals=0),
        name="near",
    )(place, inner, got_a, got_b, relay_a)
    padded = (WINDOW + 1) * nodes - (nodes - 2 * (nodes // LAYERS))
    by_layer = pl.pallas_call(
        filter_kernel,
        out_shape=jax.ShapeDtypeStruct((nodes, width), f32),
        in_specs=[SMEM] + [VMEM] * 8,
        out_specs=VMEM,
        scratch_shapes=[
            pltpu.VMEM((LAYERS, 128, 128), f32),
            pltpu.VMEM((WINDOW * LAYERS // 2, 256, 256), bf16),
            pltpu.VMEM((padded, 2 * width), bf16),
            pltpu.VMEM((padded, 2 * width), bf16),
            pltpu.VMEM((WINDOW * nodes, width), f32),
            pltpu.VMEM((WINDOW * nodes, width), f32),
        ]
        + incidence,
        compiler_params=params,
        name="filter",
    )(place, packed, inner, got_a, got_b, relay_a, relay_b, own_cells, near_cells)

    all_states = lax.all_gather(by_layer, "band", axis=1, tiled=True)
    term, filtered = pl.pallas_call(
        margin_kernel,
        out_shape=[jax.ShapeDtypeStruct((states, width), f32), jax.ShapeDtypeStruct((nodes, width), f32)],
        in_specs=[VMEM] * 5,
        out_specs=[VMEM, ANY],
        scratch_shapes=[pltpu.VMEM((nodes, width), f32), pltpu.SemaphoreType.DMA],
        compiler_params=params,
        name="margin",
    )(all_states, pick, own_pick, by_layer, back)
    rows = state_order.shape[0] // doms
    parts = lax.all_to_all(term.reshape(doms, rows, width), "dom", 0, 0, tiled=True)
    return (filtered, parts.sum(0) * (1.0 / (nodes * doms)))


def solution(mesh):
    in_specs = (P("dom", "band"), P("dom"), P("dom"), P(None, "dom"), P("dom"), P())
    out_specs = (P("dom", "band"), P("dom", "band"))
    return jax.shard_map(shards, mesh=mesh, in_specs=in_specs, out_specs=out_specs, check_vma=False)
```

```python
import functools

import jax
import jax.numpy as jnp
import numpy as np
from jax import lax
from jax.experimental import pallas as pl
from jax.experimental.pallas import tpu as pltpu
from jax.sharding import PartitionSpec as P

DEGREE = 8
REACH = 2
WINDOW = 2 * REACH + 1
LAYERS = 4
EXTRA = 24

lower_cut = 1.5
upper_edge = 5.0
anchor_value = 0.4

half_span = (upper_edge - lower_cut) / 2.0
center = (upper_edge + lower_cut) / 2.0
sigma_first = half_span / (anchor_value - center)
gamma_value = 2.0 / sigma_first


VMEM = pl.BlockSpec(memory_space=pltpu.VMEM)
SMEM = pl.BlockSpec(memory_space=pltpu.SMEM)
ANY = pl.BlockSpec(memory_space=pl.ANY)
f32 = jnp.float32
bf16 = jnp.bfloat16


def final_gain():
    sigma = gain = sigma_first
    for _ in range(DEGREE - 1):
        sigma = 1.0 / (gamma_value - sigma)
        gain = gain * 2.0 * sigma
    return gain


def dot(a, b):
    return lax.dot_general(a, b, (((1,), (0,)), ((), ())), preferred_element_type=f32)


def dot_t(a, b):
    return lax.dot_general(a, b, (((1,), (1,)), ((), ())), preferred_element_type=f32)


def split(x):
    high = x.astype(bf16)
    return high, (x - high.astype(f32)).astype(bf16)


def coarse_parts(x):
    parts = []
    for _ in range(3):
        scaled = x * float(2**19 + 1)
        part = scaled - (scaled - x)
        parts.append(part)
        x = x - part
    return parts


def exact(x):
    high, rest = x.astype(bf16), x
    terms = [high]
    for _ in range(2):
        rest = rest - terms[-1].astype(f32)
        terms.append(rest.astype(bf16))
    return terms


def cross(a, b):
    return lax.dot_general(a, b, (((0,), (0,)), ((), ())), preferred_element_type=f32)


def iota(shape, dim):
    return lax.broadcasted_iota(jnp.int32, shape, dim)


def flag(mask):
    return jnp.where(mask, 1.0, 0.0).astype(bf16)


def column_of(row):
    count = row.shape[1]
    terms = jnp.concatenate([t.astype(f32) for t in exact(row)] + [jnp.zeros((13, count), f32)], 0)
    return cross(terms.astype(bf16), jnp.ones((16, 128), bf16))


def sort_kernel(field, links, potential, mass, plane, out, rank_out, field_in, links_in, rows_in, plane_in, sems):
    nodes, width = field.shape
    copies = [
        pltpu.make_async_copy(field, field_in, sems.at[0]),
        pltpu.make_async_copy(links, links_in, sems.at[1]),
        pltpu.make_async_copy(potential, rows_in.at[pl.ds(0, 1)], sems.at[2]),
        pltpu.make_async_copy(mass, rows_in.at[pl.ds(1, 1)], sems.at[3]),
        pltpu.make_async_copy(plane, plane_in, sems.at[4]),
    ]
    for copy in copies:
        copy.start()
    for copy in copies[1:]:
        copy.wait()
    corners = links_in[...]
    corner_id = corners.astype(f32)
    plane_count = plane.shape[1]
    plane_row = jnp.concatenate([plane_in[...].astype(f32), jnp.full((1, 128 - plane_count), -1.0, f32)], 1)

    scale = lax.rsqrt(rows_in[1:2, :])
    copies[0].wait()
    field_terms = jnp.concatenate(exact(field_in[...] * column_of(scale)), 1)

    row_id = iota((nodes, nodes), 0).astype(f32)
    lane_id = iota((nodes, nodes), 1).astype(f32)
    row_small = row_id.astype(bf16)
    touched = None
    for a in range(8):
        hits = jnp.where(row_small == corner_id[a : a + 1, :].astype(bf16), jnp.ones_like(row_small), jnp.zeros_like(row_small))
        touched = hits if touched is None else touched + hits
    span = nodes // LAYERS
    by_layer = flag(iota((nodes, 128 * LAYERS), 0) // span == iota((nodes, 128 * LAYERS), 1) // 128)
    counts = dot(touched, by_layer)
    layer = [counts[:, 128 * i : 128 * (i + 1)] > 0.5 for i in range(LAYERS)]
    in_plane = flag(row_id[:, :128] == plane_row)
    is_plane = dot(in_plane, jnp.ones((128, 128), bf16)) > 0.5
    least = jnp.where(layer[0], 0.0, jnp.where(layer[1], 1.0, jnp.where(layer[2], 2.0, 3.0)))
    most = jnp.where(layer[3], 3.0, jnp.where(layer[2], 2.0, jnp.where(layer[1], 1.0, 0.0)))
    key = jnp.where(is_plane, -1.0, least + most)
    sub = iota((16, 128), 0)
    plane_facts = dot_t(
        jnp.where(sub == 0, 1.0, jnp.where(sub == 1, iota((16, 128), 1).astype(f32), 0.0)).astype(bf16), in_plane
    )
    row_counts = dot_t(flag(iota((16, nodes), 0) == iota((16, nodes), 1) // span), touched)
    row_layer = [row_counts[i : i + 1, :] > 0.5 for i in range(LAYERS)]
    row_least = jnp.where(row_layer[0], 0.0, jnp.where(row_layer[1], 1.0, jnp.where(row_layer[2], 2.0, 3.0)))
    row_most = jnp.where(row_layer[3], 3.0, jnp.where(row_layer[2], 2.0, jnp.where(row_layer[1], 1.0, 0.0)))
    key_row = jnp.where(plane_facts[0:1, :] > 0.5, -1.0, row_least + row_most)
    order_col = key * float(nodes) + row_id[:, :128]
    order_row = key_row * float(nodes) + lane_id[0:1, :]
    before = flag(jnp.concatenate([order_col] * (nodes // 128), 1) < order_row)
    counted = dot(jnp.ones((16, nodes), bf16), before)[0:1, :]
    rank = jnp.where(plane_facts[0:1, :] > 0.5, plane_facts[1:2, :], counted)
    rank_out[...] = jnp.broadcast_to(rank, rank_out.shape)

    low_lane = iota((8, 128), 1) < 64
    ranks = [jnp.broadcast_to(rank[:, 128 * h : 128 * (h + 1)], (8, 128)) for h in range(2)]
    for m in range(2):
        part = corners[:, 128 * m : 128 * (m + 1)]
        local = lax.bitwise_and(part, 127)
        found = [jnp.take_along_axis(r, local, axis=1) for r in ranks]
        place = jnp.where(part < 128, found[0], jnp.where(part < nodes, found[1], part.astype(f32)))
        place = place - jnp.where(low_lane, 128.0 * m, 128.0 * m + 64.0)
        turned = pltpu.roll(place, 64, 1)
        chance = rows_in[0:1, 128 * m : 128 * (m + 1)]
        chance = jnp.broadcast_to(chance, (8, 128))
        chance_turned = pltpu.roll(chance, 64, 1)
        for i in range(4):
            even, odd = slice(2 * i, 2 * i + 1), slice(2 * i + 1, 2 * i + 2)
            at = nodes + 8 * m + i
            out[at : at + 1, :] = jnp.where(low_lane[0:1], place[even], turned[odd])
            out[at + 4 : at + 5, :] = jnp.where(low_lane[0:1], turned[even], place[odd])
        at = nodes + 16 + 2 * m
        out[at : at + 1, :] = jnp.where(low_lane, chance, chance_turned)[0:1]
        out[at + 1 : at + 2, :] = jnp.where(low_lane, chance_turned, chance)[0:1]

    move = flag(row_id == rank)
    terms = jnp.concatenate([t.astype(f32) for t in exact(scale)] + [jnp.zeros((13, nodes), f32)], 0)
    moved = dot_t(terms.astype(bf16), move)
    scale = moved[0:1] + moved[1:2] + moved[2:3]
    out[nodes + 20 : nodes + 21, :] = scale[:, :128]
    out[nodes + 21 : nodes + 22, :] = scale[:, 128:]
    out[nodes + 22 : nodes + 24, :] = jnp.zeros((2, 128), f32)
    sorted_field = dot(move, field_terms)
    out[:nodes, :] = sorted_field[:, :width] + sorted_field[:, width : 2 * width] + sorted_field[:, 2 * width :]


def layer_matrix(table, layer, scratch):
    plain, pair, third = scratch
    low_lane = iota((1, 128), 1) < 64
    chance = table[16 + layer : 17 + layer, :]
    stiff = (0.0, 1.0 / 2.0, 1.0 / 3.0, 1.0 / 6.0)
    mass = (1.0 / 8.0, 1.0 / 24.0, 1.0 / 72.0, 1.0 / 216.0)
    whole = [(0.5 * k + chance * m) * 0.125 for k, m in zip(stiff, mass)]

    def spread(row):
        return jnp.broadcast_to(row, (16, 128)).astype(bf16)

    weights = [
        [spread(part) for part in coarse_parts(jnp.where(low_lane, whole[j], whole[j + 1]))] for j in range(3)
    ]
    rows = table[4 * layer : 4 * layer + 4, :]
    turned = pltpu.roll(table[8 * (layer // 2) : 8 * (layer // 2) + 8, :], 64, 1)
    turned = turned[4 * (layer % 2) : 4 * (layer % 2) + 4, :]
    straight = [spread(rows[i : i + 1, :]) for i in range(4)]
    opposite = [spread(turned[i : i + 1, :]) for i in range(4)]
    sign = spread(jnp.where(low_lane, 1.0, -1.0))
    one, zero = jnp.ones((16, 128), bf16), jnp.zeros((16, 128), bf16)
    for r in range(8):
        local = (iota((16, 128), 0) + 16 * r).astype(f32).astype(bf16)
        items = [
            jnp.where(local == s, sign, zero) + jnp.where(local == o, one, zero) for s, o in zip(straight, opposite)
        ]
        for bit in (1, 2):
            mixed = [None] * 4
            for i in range(4):
                if not i & bit:
                    mixed[i] = items[i] + items[i | bit]
                    mixed[i | bit] = items[i] - items[i | bit]
            items = mixed
        for i in range(4):
            part = weights[bin(i).count("1")]
            lanes = slice(128 * i, 128 * (i + 1))
            plain[16 * r : 16 * r + 16, lanes] = items[i]
            pair[16 * r : 16 * r + 16, lanes] = items[i] * part[0]
            pair[128 + 16 * r : 128 + 16 * r + 16, lanes] = items[i] * part[1]
            third[16 * r : 16 * r + 16, lanes] = items[i] * part[2]
    both = dot_t(plain[...], pair[...])
    return both[:, :128] + both[:, 128:] + dot_t(plain[...], third[...])


def partition_matrices(table, scratch, layers, out, first):
    for layer in layers:
        out[first + layer] = layer_matrix(table, layer, [ref.at[layer] for ref in scratch])


def own_kernel(place, packed, rank, order, out, back, pick, own_pick, *scratch):
    nodes, (count, width) = back.shape[0], own_pick.shape
    state_id = iota((count, count), 0)
    pick[...] = flag(state_id == order[...])
    own_order = order[:, pl.ds(pl.multiple_of(place[1] * width, width), width)]
    own_pick[...] = flag(state_id[:, :width] == own_order)
    place = jnp.concatenate([column_of(rank[0:1, :])] * (nodes // 128), 1)
    back[...] = flag(place == iota((nodes, nodes), 1).astype(f32))
    partition_matrices(packed[packed.shape[0] - EXTRA :, :], scratch, range(LAYERS), out, 0)


def around(place, inner, outer, relay_a, relay_b):
    in_four = lax.rem(place[0], 4)
    is_even = lax.rem(place[0], 2) == 0
    left1 = jnp.where(is_even, outer, inner)
    right1 = jnp.where(is_even, inner, outer)
    left2 = jnp.where(in_four < 2, relay_b, relay_a)
    right2 = jnp.where(in_four < 2, relay_a, relay_b)
    return left2, left1, right1, right2


def outer_of(place, got_a, got_b, part):
    in_four = lax.rem(place[0], 4)
    by_b = jnp.logical_or(in_four == 0, in_four == 3)
    return jnp.where(by_b, got_b[part, :], got_a[part, :])


def near_kernel(place, inner, got_a, got_b, relay_a, out, *scratch):
    nodes = inner.shape[0] - EXTRA
    part = slice(nodes, nodes + EXTRA)
    for i, table in enumerate((inner[part, :], outer_of(place, got_a, got_b, part), relay_a[part, :])):
        partition_matrices(table, scratch, range(LAYERS), out, LAYERS * i)


def filter_kernel(place, packed, inner, got_a, got_b, relay_a, relay_b, own_cells, near_cells,
                  out, far_cells, bands, even, odd, field_a, field_b, *scratch):
    nodes, width = out.shape
    span = nodes // LAYERS
    table_part, field_part = slice(nodes, nodes + EXTRA), slice(0, nodes)
    last = relay_b[table_part, :]
    partition_matrices(last, scratch, range(LAYERS), far_cells, 0)

    def window(part):
        sides = around(place, inner[part, :], outer_of(place, got_a, got_b, part), relay_a[part, :], relay_b[part, :])
        return sides[:2] + (packed[part, :],) + sides[2:]

    tables = window(table_part)
    cells = []
    for i in range(LAYERS):
        cells.append(around(place, near_cells[i], near_cells[LAYERS + i], near_cells[2 * LAYERS + i], far_cells[i]))
    cells = [cells[i][0] for i in range(4)] + [cells[i][1] for i in range(4)] + [own_cells[i] for i in range(4)] + [
        cells[i][2] for i in range(4)] + [cells[i][3] for i in range(3)] + [None]

    low_lane = iota((128, 128), 1) < span
    on_first = iota((128, 128), 1) == iota((128, 128), 0) + span
    on_second = iota((128, 128), 1) == iota((128, 128), 0) - span
    blank = jnp.zeros((span, 128), f32)
    pairs = len(cells) // 2
    for q in range(WINDOW):
        scale = column_of(jnp.concatenate([tables[q][20:21], tables[q][21:22]], 1))
        weight = scale * scale * (1.0 / half_span)
        for j in (2 * q, 2 * q + 1):
            rows = slice(128 * (j - 2 * q), 128 * (j - 2 * q) + 128)
            turned = pltpu.roll(cells[2 * j], 64, 1)
            upper = blank if j == 0 else cells[2 * j - 1][span:, :]
            lower = blank if cells[2 * j + 1] is None else cells[2 * j + 1][:span, :]
            first = jnp.concatenate([upper, blank], 0) + jnp.where(low_lane, 0.0, turned)
            second = jnp.concatenate([blank, lower], 0) + jnp.where(low_lane, turned, 0.0)
            first = first * weight[rows, :] - jnp.where(on_first, center / half_span, 0.0)
            second = second * weight[rows, :] - jnp.where(on_second, center / half_span, 0.0)
            for lanes, value in ((slice(0, 128), first), (slice(128, 256), second)):
                high, low = split(value)
                bands[j, :128, lanes] = high
                bands[j, 128:, lanes] = low

    def put(target, at, value):
        count = value.shape[0]
        high, low = split(value)
        target[span + at : span + at + count, :width] = high
        target[span + at : span + at + count, width:] = low

    for target in (even, odd):
        target[:span, :] = jnp.zeros((span, 2 * width), bf16)
        target[span + WINDOW * nodes :, :] = jnp.zeros((span, 2 * width), bf16)
    for q, value in enumerate(window(field_part)):
        field_a[nodes * q : nodes * (q + 1), :] = value
        put(even, nodes * q, value)
    final = []
    for k in range(1, DEGREE + 1):
        source, target = (even, odd) if k % 2 else (odd, even)
        newer = field_b if k % 2 else field_a
        keep = {1: None, 2: 0.5}.get(k, 0.25)
        for j in range(k // 2, pairs - k // 2):
            product = dot(bands[j], source[128 * j : 128 * j + 256, :])
            value = product[:128, :width] + (product[:128, width:] + product[128:, :width])
            if keep is not None:
                value = value - keep * newer[128 * j : 128 * (j + 1), :]
            if k == DEGREE:
                final.append(value)
            else:
                newer[128 * j : 128 * (j + 1), :] = value
                put(target, 128 * j, value)
    out[...] = jnp.concatenate(final, 0) * (final_gain() / column_of(
        jnp.concatenate([tables[REACH][20:21], tables[REACH][21:22]], 1)))


def margin_kernel(total_nodes, states, pick, own_pick, own, back, out, filtered, original, sem):
    width = out.shape[1]
    moved = dot(back[...], jnp.concatenate(exact(own[...]), 1))
    original[...] = moved[:, :width] + moved[:, width : 2 * width] + moved[:, 2 * width :]
    copy = pltpu.make_async_copy(original, filtered, sem)
    copy.start()
    high, low = split(states[...])
    own_high = dot(high, own_pick[...]).astype(bf16)
    own_low = dot(low, own_pick[...]).astype(bf16)
    part = cross(own_high, high) + cross(own_high, low) + cross(own_low, high)
    chosen = [dot(term, pick[...]) for term in exact(part)]
    out[...] = ((chosen[0] + chosen[1] + chosen[2]) * (1.0 / total_nodes)).T
    copy.wait()


def swapped(block, axis, pairs):
    count = lax.axis_size(axis)
    route = [
        step for a, b in pairs if 0 <= a and b < count for step in ((a, b), (b, a))
    ]
    return lax.ppermute(block, axis, route)


def shards(wavefunctions, node_mass, cell_potential, cell_nodes, plane_nodes, state_order):
    nodes, width = wavefunctions.shape
    doms = lax.axis_size("dom")
    place = jnp.stack([lax.axis_index("dom"), lax.axis_index("band")]).astype(jnp.int32)
    pairs = [(2 * i, 2 * i + 1) for i in range(doms)]
    fours = range(-1, doms // 4 + 1)
    mirror_a = [(4 * i + j, 4 * i + 3 - j) for i in fours for j in (0, 1)]
    mirror_b = [(4 * i + 2 + j, 4 * i + 5 - j) for i in fours for j in (0, 1)]
    params = pltpu.CompilerParams(vmem_limit_bytes=40 * 2**20)
    plane_count = plane_nodes.shape[0]

    packed, rank = pl.pallas_call(
        sort_kernel,
        out_shape=[jax.ShapeDtypeStruct((nodes + EXTRA, width), f32), jax.ShapeDtypeStruct((8, nodes), f32)],
        in_specs=[ANY] * 5,
        out_specs=[VMEM] * 2,
        scratch_shapes=[
            pltpu.VMEM((nodes, width), f32),
            pltpu.VMEM((8, nodes), jnp.int32),
            pltpu.VMEM((2, nodes), f32),
            pltpu.VMEM((1, plane_count), jnp.int32),
            pltpu.SemaphoreType.DMA((5,)),
        ],
        compiler_params=pltpu.CompilerParams(vmem_limit_bytes=60 * 2**20),
        name="sort",
    )(wavefunctions, cell_nodes, cell_potential[None, :], node_mass[None, :], plane_nodes[None, :])
    got_b, got_a, inner = [swapped(packed, "dom", route) for route in (mirror_b, mirror_a, pairs)]
    relay_a, relay_b = [swapped(block, "dom", pairs) for block in (got_a, got_b)]
    incidence = [
        pltpu.VMEM((LAYERS, 128, 512), bf16),
        pltpu.VMEM((LAYERS, 256, 512), bf16),
        pltpu.VMEM((LAYERS, 128, 512), bf16),
    ]
    states = state_order.shape[0]
    own_cells, back, pick, own_pick = pl.pallas_call(
        own_kernel,
        out_shape=[
            jax.ShapeDtypeStruct((LAYERS, 128, 128), f32),
            jax.ShapeDtypeStruct((nodes, nodes), bf16),
            jax.ShapeDtypeStruct((states, states), bf16),
            jax.ShapeDtypeStruct((states, width), bf16),
        ],
        in_specs=[SMEM] + [VMEM] * 3,
        out_specs=[VMEM] * 4,
        scratch_shapes=incidence,
        compiler_params=params,
        cost_estimate=pl.CostEstimate(flops=1_000_000_000, bytes_accessed=1_000_000, transcendentals=0),
        name="own",
    )(place, packed, rank, state_order[None, :])
    near_cells = pl.pallas_call(
        near_kernel,
        out_shape=jax.ShapeDtypeStruct((3 * LAYERS, 128, 128), f32),
        in_specs=[SMEM] + [VMEM] * 4,
        out_specs=VMEM,
        scratch_shapes=incidence,
        compiler_params=params,
        cost_estimate=pl.CostEstimate(flops=2_000_000_000, bytes_accessed=1_000_000, transcendentals=0),
        name="near",
    )(place, inner, got_a, got_b, relay_a)
    padded = (WINDOW + 1) * nodes - (nodes - 2 * (nodes // LAYERS))
    by_layer = pl.pallas_call(
        filter_kernel,
        out_shape=jax.ShapeDtypeStruct((nodes, width), f32),
        in_specs=[SMEM] + [VMEM] * 8,
        out_specs=VMEM,
        scratch_shapes=[
            pltpu.VMEM((LAYERS, 128, 128), f32),
            pltpu.VMEM((WINDOW * LAYERS // 2, 256, 256), bf16),
            pltpu.VMEM((padded, 2 * width), bf16),
            pltpu.VMEM((padded, 2 * width), bf16),
            pltpu.VMEM((WINDOW * nodes, width), f32),
            pltpu.VMEM((WINDOW * nodes, width), f32),
        ]
        + incidence,
        compiler_params=params,
        name="filter",
    )(place, packed, inner, got_a, got_b, relay_a, relay_b, own_cells, near_cells)

    all_states = lax.all_gather(by_layer, "band", axis=1, tiled=True)
    term, filtered = pl.pallas_call(
        functools.partial(margin_kernel, nodes * doms),
        out_shape=[jax.ShapeDtypeStruct((states, width), f32), jax.ShapeDtypeStruct((nodes, width), f32)],
        in_specs=[VMEM] * 5,
        out_specs=[VMEM, ANY],
        scratch_shapes=[pltpu.VMEM((nodes, width), f32), pltpu.SemaphoreType.DMA],
        compiler_params=params,
        name="margin",
    )(all_states, pick, own_pick, by_layer, back)
    rows = state_order.shape[0] // doms
    parts = lax.all_to_all(term.reshape(doms, rows, width), "dom", 0, 0, tiled=True)
    return (filtered, parts.sum(0))


def solution(mesh):
    in_specs = (P("dom", "band"), P("dom"), P("dom"), P(None, "dom"), P("dom"), P())
    out_specs = (P("dom", "band"), P("dom", "band"))
    return jax.shard_map(shards, mesh=mesh, in_specs=in_specs, out_specs=out_specs, check_vma=False)
```

```python
import jax
import jax.numpy as jnp
import numpy as np
from jax import lax
from jax.experimental import pallas as pl
from jax.experimental.pallas import tpu as pltpu
from jax.sharding import PartitionSpec as P

DEGREE = 8
REACH = 2
WINDOW = 2 * REACH + 1
LAYERS = 4
EXTRA = 24

lower_cut = 1.5
upper_edge = 5.0
anchor_value = 0.4

half_span = (upper_edge - lower_cut) / 2.0
center = (upper_edge + lower_cut) / 2.0
sigma_first = half_span / (anchor_value - center)
gamma_value = 2.0 / sigma_first


VMEM = pl.BlockSpec(memory_space=pltpu.VMEM)
SMEM = pl.BlockSpec(memory_space=pltpu.SMEM)
ANY = pl.BlockSpec(memory_space=pl.ANY)
f32 = jnp.float32
bf16 = jnp.bfloat16


def dot(a, b):
    return lax.dot_general(a, b, (((1,), (0,)), ((), ())), preferred_element_type=f32)


def dot_t(a, b):
    return lax.dot_general(a, b, (((1,), (1,)), ((), ())), preferred_element_type=f32)


def split(x):
    high = x.astype(bf16)
    return high, (x - high.astype(f32)).astype(bf16)


def coarse_parts(x):
    parts = []
    for _ in range(3):
        scaled = x * float(2**19 + 1)
        part = scaled - (scaled - x)
        parts.append(part)
        x = x - part
    return parts


def exact(x):
    high, rest = x.astype(bf16), x
    terms = [high]
    for _ in range(2):
        rest = rest - terms[-1].astype(f32)
        terms.append(rest.astype(bf16))
    return terms


def cross(a, b):
    return lax.dot_general(a, b, (((0,), (0,)), ((), ())), preferred_element_type=f32)


def iota(shape, dim):
    return lax.broadcasted_iota(jnp.int32, shape, dim)


def flag(mask):
    return jnp.where(mask, 1.0, 0.0).astype(bf16)


def column_of(row):
    count = row.shape[1]
    terms = jnp.concatenate([t.astype(f32) for t in exact(row)] + [jnp.zeros((13, count), f32)], 0)
    return cross(terms.astype(bf16), jnp.ones((16, 128), bf16))


def sort_kernel(field, links, potential, mass, plane, out, rank_out, field_in, links_in, rows_in, plane_in, sems):
    nodes, width = field.shape
    copies = [
        pltpu.make_async_copy(field, field_in, sems.at[0]),
        pltpu.make_async_copy(links, links_in, sems.at[1]),
        pltpu.make_async_copy(potential, rows_in.at[pl.ds(0, 1)], sems.at[2]),
        pltpu.make_async_copy(mass, rows_in.at[pl.ds(1, 1)], sems.at[3]),
        pltpu.make_async_copy(plane, plane_in, sems.at[4]),
    ]
    for copy in copies:
        copy.start()
    for copy in copies[1:]:
        copy.wait()
    corners = links_in[...]
    corner_id = corners.astype(f32)
    plane_count = plane.shape[1]
    plane_row = jnp.concatenate([plane_in[...].astype(f32), jnp.full((1, 128 - plane_count), -1.0, f32)], 1)

    row_id = iota((nodes, nodes), 0).astype(f32)
    lane_id = iota((nodes, nodes), 1).astype(f32)
    row_small = row_id.astype(bf16)
    touched = None
    for a in range(8):
        hits = jnp.where(row_small == corner_id[a : a + 1, :].astype(bf16), jnp.ones_like(row_small), jnp.zeros_like(row_small))
        touched = hits if touched is None else touched + hits
    span = nodes // LAYERS
    by_layer = flag(iota((nodes, 128 * LAYERS), 0) // span == iota((nodes, 128 * LAYERS), 1) // 128)
    counts = dot(touched, by_layer)
    layer = [counts[:, 128 * i : 128 * (i + 1)] > 0.5 for i in range(LAYERS)]
    in_plane = flag(row_id[:, :128] == plane_row)
    is_plane = dot(in_plane, jnp.ones((128, 128), bf16)) > 0.5
    least = jnp.where(layer[0], 0.0, jnp.where(layer[1], 1.0, jnp.where(layer[2], 2.0, 3.0)))
    most = jnp.where(layer[3], 3.0, jnp.where(layer[2], 2.0, jnp.where(layer[1], 1.0, 0.0)))
    key = jnp.where(is_plane, -1.0, least + most)
    sub = iota((16, 128), 0)
    plane_facts = dot_t(
        jnp.where(sub == 0, 1.0, jnp.where(sub == 1, iota((16, 128), 1).astype(f32), 0.0)).astype(bf16), in_plane
    )
    row_counts = dot_t(flag(iota((16, nodes), 0) == iota((16, nodes), 1) // span), touched)
    row_layer = [row_counts[i : i + 1, :] > 0.5 for i in range(LAYERS)]
    row_least = jnp.where(row_layer[0], 0.0, jnp.where(row_layer[1], 1.0, jnp.where(row_layer[2], 2.0, 3.0)))
    row_most = jnp.where(row_layer[3], 3.0, jnp.where(row_layer[2], 2.0, jnp.where(row_layer[1], 1.0, 0.0)))
    key_row = jnp.where(plane_facts[0:1, :] > 0.5, -1.0, row_least + row_most)
    order_col = key * float(nodes) + row_id[:, :128]
    order_row = key_row * float(nodes) + lane_id[0:1, :]
    before = flag(jnp.concatenate([order_col] * (nodes // 128), 1) < order_row)
    counted = dot(jnp.ones((16, nodes), bf16), before)[0:1, :]
    rank = jnp.where(plane_facts[0:1, :] > 0.5, plane_facts[1:2, :], counted)
    rank_out[...] = jnp.broadcast_to(rank, rank_out.shape)

    low_lane = iota((8, 128), 1) < 64
    ranks = [jnp.broadcast_to(rank[:, 128 * h : 128 * (h + 1)], (8, 128)) for h in range(2)]
    for m in range(2):
        part = corners[:, 128 * m : 128 * (m + 1)]
        local = lax.bitwise_and(part, 127)
        found = [jnp.take_along_axis(r, local, axis=1) for r in ranks]
        place = jnp.where(part < 128, found[0], jnp.where(part < nodes, found[1], part.astype(f32)))
        place = place - jnp.where(low_lane, 128.0 * m, 128.0 * m + 64.0)
        turned = pltpu.roll(place, 64, 1)
        chance = rows_in[0:1, 128 * m : 128 * (m + 1)]
        chance = jnp.broadcast_to(chance, (8, 128))
        chance_turned = pltpu.roll(chance, 64, 1)
        for i in range(4):
            even, odd = slice(2 * i, 2 * i + 1), slice(2 * i + 1, 2 * i + 2)
            at = nodes + 8 * m + i
            out[at : at + 1, :] = jnp.where(low_lane[0:1], place[even], turned[odd])
            out[at + 4 : at + 5, :] = jnp.where(low_lane[0:1], turned[even], place[odd])
        at = nodes + 16 + 2 * m
        out[at : at + 1, :] = jnp.where(low_lane, chance, chance_turned)[0:1]
        out[at + 1 : at + 2, :] = jnp.where(low_lane, chance_turned, chance)[0:1]

    move = flag(row_id == rank)
    scale = lax.rsqrt(rows_in[1:2, :])
    terms = jnp.concatenate([t.astype(f32) for t in exact(scale)] + [jnp.zeros((13, nodes), f32)], 0)
    moved = dot_t(terms.astype(bf16), move)
    scale = moved[0:1] + moved[1:2] + moved[2:3]
    out[nodes + 20 : nodes + 21, :] = scale[:, :128]
    out[nodes + 21 : nodes + 22, :] = scale[:, 128:]
    out[nodes + 22 : nodes + 24, :] = jnp.zeros((2, 128), f32)
    copies[0].wait()
    sorted_field = dot(move, jnp.concatenate(exact(field_in[...]), 1))
    sorted_field = sorted_field[:, :width] + sorted_field[:, width : 2 * width] + sorted_field[:, 2 * width :]
    out[:nodes, :] = sorted_field * column_of(scale)


def layer_matrix(table, layer, scratch):
    plain, pair, third = scratch
    low_lane = iota((1, 128), 1) < 64
    chance = table[16 + layer : 17 + layer, :]
    stiff = (0.0, 1.0 / 2.0, 1.0 / 3.0, 1.0 / 6.0)
    mass = (1.0 / 8.0, 1.0 / 24.0, 1.0 / 72.0, 1.0 / 216.0)
    whole = [(0.5 * k + chance * m) * 0.125 for k, m in zip(stiff, mass)]

    def spread(row):
        return jnp.broadcast_to(row, (16, 128)).astype(bf16)

    weights = [
        [spread(part) for part in coarse_parts(jnp.where(low_lane, whole[j], whole[j + 1]))] for j in range(3)
    ]
    rows = table[4 * layer : 4 * layer + 4, :]
    turned = pltpu.roll(table[8 * (layer // 2) : 8 * (layer // 2) + 8, :], 64, 1)
    turned = turned[4 * (layer % 2) : 4 * (layer % 2) + 4, :]
    straight = [spread(rows[i : i + 1, :]) for i in range(4)]
    opposite = [spread(turned[i : i + 1, :]) for i in range(4)]
    sign = spread(jnp.where(low_lane, 1.0, -1.0))
    one, zero = jnp.ones((16, 128), bf16), jnp.zeros((16, 128), bf16)
    for r in range(8):
        local = (iota((16, 128), 0) + 16 * r).astype(f32).astype(bf16)
        items = [
            jnp.where(local == s, sign, zero) + jnp.where(local == o, one, zero) for s, o in zip(straight, opposite)
        ]
        for bit in (1, 2):
            mixed = [None] * 4
            for i in range(4):
                if not i & bit:
                    mixed[i] = items[i] + items[i | bit]
                    mixed[i | bit] = items[i] - items[i | bit]
            items = mixed
        for i in range(4):
            part = weights[bin(i).count("1")]
            lanes = slice(128 * i, 128 * (i + 1))
            plain[16 * r : 16 * r + 16, lanes] = items[i]
            pair[16 * r : 16 * r + 16, lanes] = items[i] * part[0]
            pair[128 + 16 * r : 128 + 16 * r + 16, lanes] = items[i] * part[1]
            third[16 * r : 16 * r + 16, lanes] = items[i] * part[2]
    both = dot_t(plain[...], pair[...])
    return both[:, :128] + both[:, 128:] + dot_t(plain[...], third[...])


def partition_matrices(table, scratch, layers, out, first):
    for layer in layers:
        out[first + layer] = layer_matrix(table, layer, [ref.at[layer] for ref in scratch])


def own_kernel(place, packed, rank, order, out, back, pick, own_pick, *scratch):
    nodes, (count, width) = back.shape[0], own_pick.shape
    state_id = iota((count, count), 0)
    pick[...] = flag(state_id == order[...])
    own_order = order[:, pl.ds(pl.multiple_of(place[1] * width, width), width)]
    own_pick[...] = flag(state_id[:, :width] == own_order)
    place = jnp.concatenate([column_of(rank[0:1, :])] * (nodes // 128), 1)
    back[...] = flag(place == iota((nodes, nodes), 1).astype(f32))
    partition_matrices(packed[packed.shape[0] - EXTRA :, :], scratch, range(LAYERS), out, 0)


def around(place, inner, outer, relay_a, relay_b):
    in_four = lax.rem(place[0], 4)
    is_even = lax.rem(place[0], 2) == 0
    left1 = jnp.where(is_even, outer, inner)
    right1 = jnp.where(is_even, inner, outer)
    left2 = jnp.where(in_four < 2, relay_b, relay_a)
    right2 = jnp.where(in_four < 2, relay_a, relay_b)
    return left2, left1, right1, right2


def outer_of(place, got_a, got_b, part):
    in_four = lax.rem(place[0], 4)
    by_b = jnp.logical_or(in_four == 0, in_four == 3)
    return jnp.where(by_b, got_b[part, :], got_a[part, :])


def near_kernel(place, inner, got_a, got_b, relay_a, out, *scratch):
    nodes = inner.shape[0] - EXTRA
    part = slice(nodes, nodes + EXTRA)
    for i, table in enumerate((inner[part, :], outer_of(place, got_a, got_b, part), relay_a[part, :])):
        partition_matrices(table, scratch, range(LAYERS), out, LAYERS * i)


def filter_kernel(place, packed, inner, got_a, got_b, relay_a, relay_b, own_cells, near_cells,
                  out, far_cells, bands, even, odd, field_a, field_b, *scratch):
    nodes, width = out.shape
    span = nodes // LAYERS
    table_part, field_part = slice(nodes, nodes + EXTRA), slice(0, nodes)
    last = relay_b[table_part, :]
    partition_matrices(last, scratch, range(LAYERS), far_cells, 0)

    def window(part):
        sides = around(place, inner[part, :], outer_of(place, got_a, got_b, part), relay_a[part, :], relay_b[part, :])
        return sides[:2] + (packed[part, :],) + sides[2:]

    tables = window(table_part)
    cells = []
    for i in range(LAYERS):
        cells.append(around(place, near_cells[i], near_cells[LAYERS + i], near_cells[2 * LAYERS + i], far_cells[i]))
    cells = [cells[i][0] for i in range(4)] + [cells[i][1] for i in range(4)] + [own_cells[i] for i in range(4)] + [
        cells[i][2] for i in range(4)] + [cells[i][3] for i in range(3)] + [None]

    low_lane = iota((128, 128), 1) < span
    on_first = iota((128, 128), 1) == iota((128, 128), 0) + span
    on_second = iota((128, 128), 1) == iota((128, 128), 0) - span
    blank = jnp.zeros((span, 128), f32)
    pairs = len(cells) // 2
    for q in range(WINDOW):
        scale = column_of(jnp.concatenate([tables[q][20:21], tables[q][21:22]], 1))
        weight = scale * scale * (1.0 / half_span)
        for j in (2 * q, 2 * q + 1):
            rows = slice(128 * (j - 2 * q), 128 * (j - 2 * q) + 128)
            turned = pltpu.roll(cells[2 * j], 64, 1)
            upper = blank if j == 0 else cells[2 * j - 1][span:, :]
            lower = blank if cells[2 * j + 1] is None else cells[2 * j + 1][:span, :]
            first = jnp.concatenate([upper, blank], 0) + jnp.where(low_lane, 0.0, turned)
            second = jnp.concatenate([blank, lower], 0) + jnp.where(low_lane, turned, 0.0)
            first = first * weight[rows, :] - jnp.where(on_first, center / half_span, 0.0)
            second = second * weight[rows, :] - jnp.where(on_second, center / half_span, 0.0)
            for lanes, value in ((slice(0, 128), first), (slice(128, 256), second)):
                high, low = split(value)
                bands[j, :128, lanes] = high
                bands[j, 128:, lanes] = low

    def put(target, at, value):
        count = value.shape[0]
        high, low = split(value)
        target[span + at : span + at + count, :width] = high
        target[span + at : span + at + count, width:] = low

    for target in (even, odd):
        target[:span, :] = jnp.zeros((span, 2 * width), bf16)
        target[span + WINDOW * nodes :, :] = jnp.zeros((span, 2 * width), bf16)
    for q, value in enumerate(window(field_part)):
        field_a[nodes * q : nodes * (q + 1), :] = value
        put(even, nodes * q, value)
    sigma_last = sigma_first
    final = []
    for k in range(1, DEGREE + 1):
        source, target = (even, odd) if k % 2 else (odd, even)
        newer = field_b if k % 2 else field_a
        if k == 1:
            gain, keep = sigma_first, None
        else:
            sigma_next = 1.0 / (gamma_value - sigma_last)
            gain, keep = 2.0 * sigma_next, sigma_last * sigma_next
            sigma_last = sigma_next
        for j in range(k // 2, pairs - k // 2):
            product = dot(bands[j], source[128 * j : 128 * j + 256, :])
            value = gain * (product[:128, :width] + (product[:128, width:] + product[128:, :width]))
            if keep is not None:
                value = value - keep * newer[128 * j : 128 * (j + 1), :]
            if k == DEGREE:
                final.append(value)
            else:
                newer[128 * j : 128 * (j + 1), :] = value
                put(target, 128 * j, value)
    scale = column_of(jnp.concatenate([tables[REACH][20:21], tables[REACH][21:22]], 1))
    out[...] = jnp.concatenate(final, 0) / scale


def margin_kernel(states, pick, own_pick, own, back, out, filtered, original, sem):
    width = out.shape[1]
    moved = dot(back[...], jnp.concatenate(exact(own[...]), 1))
    original[...] = moved[:, :width] + moved[:, width : 2 * width] + moved[:, 2 * width :]
    copy = pltpu.make_async_copy(original, filtered, sem)
    copy.start()
    high, low = split(states[...])
    own_high = dot(high, own_pick[...]).astype(bf16)
    own_low = dot(low, own_pick[...]).astype(bf16)
    part = cross(own_high, high) + cross(own_high, low) + cross(own_low, high)
    chosen = [dot(term, pick[...]) for term in split(part)]
    out[...] = (chosen[0] + chosen[1]).T
    copy.wait()


def swapped(block, axis, pairs):
    count = lax.axis_size(axis)
    route = [
        step for a, b in pairs if 0 <= a and b < count for step in ((a, b), (b, a))
    ]
    return lax.ppermute(block, axis, route)


def shards(wavefunctions, node_mass, cell_potential, cell_nodes, plane_nodes, state_order):
    nodes, width = wavefunctions.shape
    doms = lax.axis_size("dom")
    place = jnp.stack([lax.axis_index("dom"), lax.axis_index("band")]).astype(jnp.int32)
    pairs = [(2 * i, 2 * i + 1) for i in range(doms)]
    fours = range(-1, doms // 4 + 1)
    mirror_a = [(4 * i + j, 4 * i + 3 - j) for i in fours for j in (0, 1)]
    mirror_b = [(4 * i + 2 + j, 4 * i + 5 - j) for i in fours for j in (0, 1)]
    params = pltpu.CompilerParams(vmem_limit_bytes=40 * 2**20)
    plane_count = plane_nodes.shape[0]

    packed, rank = pl.pallas_call(
        sort_kernel,
        out_shape=[jax.ShapeDtypeStruct((nodes + EXTRA, width), f32), jax.ShapeDtypeStruct((8, nodes), f32)],
        in_specs=[ANY] * 5,
        out_specs=[VMEM] * 2,
        scratch_shapes=[
            pltpu.VMEM((nodes, width), f32),
            pltpu.VMEM((8, nodes), jnp.int32),
            pltpu.VMEM((2, nodes), f32),
            pltpu.VMEM((1, plane_count), jnp.int32),
            pltpu.SemaphoreType.DMA((5,)),
        ],
        compiler_params=pltpu.CompilerParams(vmem_limit_bytes=60 * 2**20),
        name="sort",
    )(wavefunctions, cell_nodes, cell_potential[None, :], node_mass[None, :], plane_nodes[None, :])
    got_b, got_a, inner = [swapped(packed, "dom", route) for route in (mirror_b, mirror_a, pairs)]
    relay_a, relay_b = [swapped(block, "dom", pairs) for block in (got_a, got_b)]
    incidence = [
        pltpu.VMEM((LAYERS, 128, 512), bf16),
        pltpu.VMEM((LAYERS, 256, 512), bf16),
        pltpu.VMEM((LAYERS, 128, 512), bf16),
    ]
    states = state_order.shape[0]
    own_cells, back, pick, own_pick = pl.pallas_call(
        own_kernel,
        out_shape=[
            jax.ShapeDtypeStruct((LAYERS, 128, 128), f32),
            jax.ShapeDtypeStruct((nodes, nodes), bf16),
            jax.ShapeDtypeStruct((states, states), bf16),
            jax.ShapeDtypeStruct((states, width), bf16),
        ],
        in_specs=[SMEM] + [VMEM] * 3,
        out_specs=[VMEM] * 4,
        scratch_shapes=incidence,
        compiler_params=params,
        cost_estimate=pl.CostEstimate(flops=1_000_000_000, bytes_accessed=1_000_000, transcendentals=0),
        name="own",
    )(place, packed, rank, state_order[None, :])
    near_cells = pl.pallas_call(
        near_kernel,
        out_shape=jax.ShapeDtypeStruct((3 * LAYERS, 128, 128), f32),
        in_specs=[SMEM] + [VMEM] * 4,
        out_specs=VMEM,
        scratch_shapes=incidence,
        compiler_params=params,
        cost_estimate=pl.CostEstimate(flops=2_000_000_000, bytes_accessed=1_000_000, transcendentals=0),
        name="near",
    )(place, inner, got_a, got_b, relay_a)
    padded = (WINDOW + 1) * nodes - (nodes - 2 * (nodes // LAYERS))
    by_layer = pl.pallas_call(
        filter_kernel,
        out_shape=jax.ShapeDtypeStruct((nodes, width), f32),
        in_specs=[SMEM] + [VMEM] * 8,
        out_specs=VMEM,
        scratch_shapes=[
            pltpu.VMEM((LAYERS, 128, 128), f32),
            pltpu.VMEM((WINDOW * LAYERS // 2, 256, 256), bf16),
            pltpu.VMEM((padded, 2 * width), bf16),
            pltpu.VMEM((padded, 2 * width), bf16),
            pltpu.VMEM((WINDOW * nodes, width), f32),
            pltpu.VMEM((WINDOW * nodes, width), f32),
        ]
        + incidence,
        compiler_params=params,
        name="filter",
    )(place, packed, inner, got_a, got_b, relay_a, relay_b, own_cells, near_cells)

    all_states = lax.all_gather(by_layer, "band", axis=1, tiled=True)
    term, filtered = pl.pallas_call(
        margin_kernel,
        out_shape=[jax.ShapeDtypeStruct((states, width), f32), jax.ShapeDtypeStruct((nodes, width), f32)],
        in_specs=[VMEM] * 5,
        out_specs=[VMEM, ANY],
        scratch_shapes=[pltpu.VMEM((nodes, width), f32), pltpu.SemaphoreType.DMA],
        compiler_params=params,
        name="margin",
    )(all_states, pick, own_pick, by_layer, back)
    rows = state_order.shape[0] // doms
    parts = lax.all_to_all(term.reshape(doms, rows, width), "dom", 0, 0, tiled=True)
    return (filtered, parts.sum(0) * (1.0 / (nodes * doms)))


def solution(mesh):
    in_specs = (P("dom", "band"), P("dom"), P("dom"), P(None, "dom"), P("dom"), P())
    out_specs = (P("dom", "band"), P("dom", "band"))
    return jax.shard_map(shards, mesh=mesh, in_specs=in_specs, out_specs=out_specs, check_vma=False)
```
